32 devices in a mesh: parts: 2 (over x), slab: 16 (over z, y, core).
Axes of the slice: x: 2, y: 2, z: 4, core: 2. Of those that a mesh axis runs over, the one named last changes fastest.
Arguments:
- features: bfloat16 [32768, 64], P(('parts', 'slab')), parts along dimension 0, may hold values from -6 to 6
- weight_one: bfloat16 [27, 64, 64], replicated, may hold values from -0.21875 to 0.21875
- weight_two: bfloat16 [27, 64, 64], replicated, may hold values from -0.21875 to 0.21875
- rules: int32 [32768, 27], P(('parts', 'slab')), parts along dimension 0, may hold values from -1 to 1535, as said below
- cotangent: bfloat16 [32768, 64], P(('parts', 'slab')), parts along dimension 0, may hold values from -6 to 6
Outputs:
- features_grad: bfloat16 [32768, 64], P(('parts', 'slab')), parts along dimension 0
- grad_one: float32 [54, 64, 64], P('parts'), parts along dimension 0
- grad_two: float32 [54, 64, 64], P('parts'), parts along dimension 0
The draws below stay inside these ranges and needn't reach their ends.
There are 2 independent parts, one for each index of `parts`. The reference program is written for one: setup_inputs(seed, part) draws one part's arguments, and reference() takes and returns one part's arrays. A program takes and returns all parts, laid end to end along the dimension named above; an argument that names none is the same for every part. Nothing has to cross between parts.
Inputs may be any that keep to these rules, and one draw needn't show every extreme that they name: `rules`: the rows of an owner block are the cells of a box of 4 planes of 16 x 16 cells, plane by plane along the slab, then row by row; owner blocks follow one another along the slab. Offset k = 9 (dz + 1) + 3 (dy + 1) + (dx + 1) of the cell at (z, y, x) holds 256 + (z + dz) * 256 + (y + dy) * 16 + (x + dx) when the cell and its neighbour at (z + dz, y + dy, x + dx) are both occupied and the neighbour lies inside the slab window's cross section, else -1; unoccupied cells hold -1 at every offset. The occupied share differs from owner to owner, and some owner is fully occupied.
All inputs are finite; a program needn't handle non-finite values.
Results may differ from the reference program's by a relative error of at most 0.0049.
Values may be sent and summed in bfloat16 or wider, within the bound.
No kernel may reach another device: no remote copies, remote signals or barrier semaphores. Data moves between devices by JAX's collectives and lax.ppermute only.
A program may use at most 64 MiB of HBM per device.

```python
import jax
import jax.numpy as jnp
from jax import lax

CH = 64
KOFF = 27
SIDE = 16
DEPTH = 4
ROWS_DEV = 1024
RIM = 256
ROWS = 16384
N_SLAB = 16


def draw_rules(key, part):
    key = jax.random.fold_in(key, 7)
    key_rate, key_full, key_occ = jax.random.split(key, 3)
    owners = ROWS // ROWS_DEV
    rates = jax.random.randint(key_rate, (owners,), 256, 1025)
    full = jax.random.randint(key_full, (), 0, owners - 1)
    owner_ids = jnp.arange(owners)
    rates = jnp.where(owner_ids == full, 1024, rates)
    coins = jax.random.randint(key_occ, (owners, DEPTH, SIDE, SIDE), 0, 1024)
    occupied = coins < rates[:, None, None, None]
    zpos = jnp.arange(DEPTH, dtype=jnp.int32)[:, None, None]
    ypos = jnp.arange(SIDE, dtype=jnp.int32)[None, :, None]
    xpos = jnp.arange(SIDE, dtype=jnp.int32)[None, None, :]
    corner = (zpos == 0) & (ypos == SIDE - 1) & (xpos == SIDE - 1)
    forced = (owner_ids == full + 1)[:, None, None, None] & corner[None]
    occupied = occupied | forced
    flat = occupied.reshape(owners * DEPTH, SIDE, SIDE)
    padded = jnp.pad(flat, ((1, 1), (1, 1), (1, 1)))
    columns = []
    for dz in (-1, 0, 1):
        for dy in (-1, 0, 1):
            for dx in (-1, 0, 1):
                near = padded[1 + dz:1 + dz + owners * DEPTH, 1 + dy:1 + dy + SIDE, 1 + dx:1 + dx + SIDE]
                near = near.reshape(owners, DEPTH, SIDE, SIDE)
                source = RIM + (zpos + dz) * RIM + (ypos + dy) * SIDE + (xpos + dx)
                source = jnp.broadcast_to(source[None], (owners, DEPTH, SIDE, SIDE))
                columns.append(jnp.where(occupied & near, source, -1))
    rules = jnp.stack(columns, -1)
    return rules.astype(jnp.int32).reshape(ROWS, KOFF)


def steps_of(key, extent, shards, least, largest):
    loudness, own = 1.0, jax.random.fold_in(key, 6)
    for position, parts in shards:
        steps = jnp.exp(jax.random.uniform(jax.random.fold_in(own, position), (parts,), jnp.float32, least / len(shards), largest / len(shards)))
        loudness = loudness * jnp.repeat(steps, extent[position] // parts).reshape([-1 if axis == position else 1 for axis in range(len(extent))])
    return loudness


def scatter_about(key, extent, spread, limit, shards=(), kind=jnp.bfloat16):
    gain = steps_of(key, extent, shards, -0.22, 0.18) if shards else 1.0
    drawn = jax.random.normal(key, extent, jnp.float32) * spread * gain
    return jnp.minimum(jnp.maximum(drawn, -limit), limit).astype(kind)


def setup_inputs(seed: int = 0, part: int = 0) -> dict:
    streams_of = jax.random.split(jax.random.key(seed), 6)
    part_keys = jax.random.split(jax.random.fold_in(streams_of[5], part), 6)
    return {
        "features": scatter_about(part_keys[0], (ROWS, CH), 1.0, 6.0, ((0, 16),)),
        "weight_one": scatter_about(streams_of[1], (KOFF, CH, CH), (KOFF * CH // 2) ** -0.5, 0.21875),
        "weight_two": scatter_about(streams_of[2], (KOFF, CH, CH), (KOFF * CH // 2) ** -0.5, 0.21875),
        "rules": draw_rules(jax.random.fold_in(jax.random.fold_in(streams_of[5], part), 71), part),
        "cotangent": scatter_about(part_keys[4], (ROWS, CH), 1.0, 6.0, ((0, 16),)),
    }


def extend(blocks):
    zero = jnp.zeros_like(blocks[:1, :RIM])
    left = jnp.concatenate([zero, blocks[:-1, ROWS_DEV - RIM:]], 0)
    right = jnp.concatenate([blocks[1:, :RIM], zero], 0)
    return jnp.concatenate([left, blocks, right], 1)


def collect(extended, rule):
    taken = jnp.take(extended, jnp.maximum(rule, 0), axis=0)
    taken = jnp.where((rule >= 0)[:, :, None], taken, jnp.zeros((), extended.dtype))
    return taken.reshape(rule.shape[0], -1)


def spread_block(rule, grads, wflat):
    terms = jnp.dot(grads, wflat.T, preferred_element_type=jnp.float32).reshape(-1, CH)
    span = ROWS_DEV + 2 * RIM
    target = jnp.where(rule >= 0, rule, span).reshape(-1)
    return jax.ops.segment_sum(terms, target, num_segments=span + 1)[:span]


def fold_back(extended):
    middle = extended[:, RIM:RIM + ROWS_DEV]
    zero = jnp.zeros_like(extended[:1, :RIM])
    from_left = jnp.concatenate([zero, extended[:-1, RIM + ROWS_DEV:]], 0)
    from_right = jnp.concatenate([extended[1:, :RIM], zero], 0)
    middle = middle.at[:, :RIM].add(from_left)
    middle = middle.at[:, ROWS_DEV - RIM:].add(from_right)
    return middle


def weight_total(extended, rule_b, grads_b):
    def step(total, item):
        ext, rule, grads = item
        gathered = collect(ext, rule)
        term = lax.dot_general(gathered, grads, (((0,), (0,)), ((), ())), preferred_element_type=jnp.float32)
        return total + term, None
    total, _ = lax.scan(step, jnp.zeros((KOFF * CH, CH), jnp.float32), (extended, rule_b, grads_b))
    return total


def reference(features, weight_one, weight_two, rules, cotangent):
    blocks = features.reshape(N_SLAB, ROWS_DEV, CH)
    rule_b = rules.reshape(N_SLAB, ROWS_DEV, KOFF)
    cot = cotangent.reshape(N_SLAB, ROWS_DEV, CH)
    w_first = weight_one.reshape(KOFF * CH, CH)
    w_second = weight_two.reshape(KOFF * CH, CH)
    ext_in = extend(blocks)
    pre = lax.map(lambda item: jnp.dot(collect(item[0], item[1]), w_first, preferred_element_type=jnp.float32), (ext_in, rule_b))
    hidden = jax.nn.silu(pre).astype(jnp.bfloat16)
    ext_hidden = extend(hidden)
    grad_two = weight_total(ext_hidden, rule_b, cot)
    spread_two = lax.map(lambda item: spread_block(item[0], item[1], w_second), (rule_b, cot))
    hidden_grad = fold_back(spread_two)
    sig = jax.nn.sigmoid(pre)
    pre_grad = (hidden_grad * sig * (1.0 + pre * (1.0 - sig))).astype(jnp.bfloat16)
    grad_one = weight_total(ext_in, rule_b, pre_grad)
    spread_one = lax.map(lambda item: spread_block(item[0], item[1], w_first), (rule_b, pre_grad))
    features_grad = fold_back(spread_one).reshape(ROWS, CH).astype(jnp.bfloat16)
    return features_grad, grad_one.reshape(KOFF, CH, CH), grad_two.reshape(KOFF, CH, CH)
```

```python
import functools

import jax
import jax.numpy as jnp
from jax import lax
from jax.experimental import pallas as pl
from jax.experimental.pallas import tpu as pltpu
from jax.sharding import PartitionSpec as P

SIDE = 16
RIM = SIDE * SIDE
BF = jnp.bfloat16
F32 = jnp.float32
OFFSETS = [dy * SIDE + dx for dy in (-1, 0, 1) for dx in (-1, 0, 1)]


def edge_masks(length):
    lane = lax.broadcasted_iota(jnp.int32, (1, length), 1)
    x, y = lane % SIDE, (lane // SIDE) % SIDE
    inside = {}
    for dy in (-1, 0, 1):
        for dx in (-1, 0, 1):
            ok = (x + dx >= 0) & (x + dx < SIDE) & (y + dy >= 0) & (y + dy < SIDE)
            inside[dy * SIDE + dx] = jnp.where(ok, 1.0, 0.0).astype(BF)
    return inside


def write_shifts(dst, values):
    length = values.shape[1]
    inside = edge_masks(length)
    chans = values.shape[0]
    for j, off in enumerate(OFFSETS):
        moved = values if off == 0 else pltpu.roll(values, (-off) % length, 1) * inside[off]
        dst[j * chans : (j + 1) * chans, :] = moved


def dot(a, b, ca, cb):
    return lax.dot_general(a, b, (((ca,), (cb,)), ((), ())), preferred_element_type=F32)


def join_planes(terms, chans):
    n = terms.shape[1]
    return (
        terms[:chans, : n - 2 * RIM]
        + terms[chans : 2 * chans, RIM : n - RIM]
        + terms[2 * chans :, 2 * RIM :]
    )


def backward_weights(w_ref, dst, chans):
    for dz in range(3):
        for j in range(9):
            dst[dz * chans : (dz + 1) * chans, j * chans : (j + 1) * chans] = w_ref[26 - (dz * 9 + j)]


def forward_weights(w_ref, dst, chans):
    for dz in range(3):
        for j in range(9):
            dst[j * chans : (j + 1) * chans, dz * chans : (dz + 1) * chans] = w_ref[dz * 9 + j]


def prep_kernel(f_ref, c_ref, r_ref, low_ref, high_ref):
    n = f_ref.shape[1]
    chans = f_ref.shape[0]
    mask = jnp.where(r_ref[5:6, :] >= 0, 1.0, 0.0).astype(BF)
    for ref, start in ((low_ref, 0), (high_ref, n - 2 * RIM)):
        m = mask[:, start : start + 2 * RIM]
        ref[:chans, :] = f_ref[:, start : start + 2 * RIM] * m
        ref[chans : 2 * chans, :] = c_ref[:, start : start + 2 * RIM] * m
        ref[2 * chans :, :] = jnp.broadcast_to(m, (16, 2 * RIM))


def main_kernel(f_ref, c_ref, r_ref, left_ref, right_ref, w1_ref, w2_ref, pg_ref, grads_ref,
                s_f, s_c, wf, wb):
    chans, n = f_ref.shape
    mask = jnp.where(r_ref[5:6, :] >= 0, 1.0, 0.0).astype(BF)
    ext_m = jnp.concatenate(
        [left_ref[2 * chans : 2 * chans + 1, RIM:], mask, right_ref[2 * chans : 2 * chans + 1, :RIM]], 1
    ).astype(F32)
    ext_f = jnp.concatenate([left_ref[:chans, :], f_ref[...] * mask, right_ref[:chans, :]], 1)
    ext_c = jnp.concatenate(
        [left_ref[chans : 2 * chans, :], c_ref[...] * mask, right_ref[chans : 2 * chans, :]], 1
    )
    write_shifts(s_f, ext_f)
    write_shifts(s_c, ext_c)
    forward_weights(w1_ref, wf, chans)
    backward_weights(w2_ref, wb, chans)
    pre = join_planes(dot(wf[...], s_f[...], 0, 0), chans)
    sig = 1.0 / (1.0 + jnp.exp(-pre))
    hidden = (pre * sig * ext_m).astype(BF)[:, RIM : RIM + n]
    blank = jnp.zeros((chans, 2 * RIM), BF)
    hid = jnp.concatenate([blank, hidden, blank], 1)
    hid3 = jnp.concatenate([hid[:, (2 - d) * RIM : (2 - d) * RIM + n + 2 * RIM] for d in range(3)], 0)
    g2 = dot(hid3, s_c[:, RIM : n + 3 * RIM], 1, 1)
    hg = join_planes(dot(wb[...], s_c[...], 1, 0), chans) * ext_m
    pg = (hg * sig * (1.0 + pre * (1.0 - sig))).astype(BF)
    pg_ref[...] = pg
    own = jnp.concatenate([blank, pg[:, RIM : RIM + n], blank], 1)
    own3 = jnp.concatenate([own[:, (2 - d) * RIM : (2 - d) * RIM + n + 2 * RIM] for d in range(3)], 0)
    g1 = dot(s_f[:, RIM : n + 3 * RIM], own3, 1, 1)
    for dz in range(3):
        for j in range(9):
            k = dz * 9 + j
            r = 26 - k
            bz, bj = r // 9, r % 9
            grads_ref[k * chans : (k + 1) * chans, :chans] = g1[
                j * chans : (j + 1) * chans, dz * chans : (dz + 1) * chans
            ]
            grads_ref[k * chans : (k + 1) * chans, chans:] = g2[
                bz * chans : (bz + 1) * chans, bj * chans : (bj + 1) * chans
            ]


def last_kernel(pg_ref, r_ref, w1_ref, out_ref, s_p, wb):
    chans = w1_ref.shape[1]
    mask = jnp.where(r_ref[5:6, :] >= 0, 1.0, 0.0)
    write_shifts(s_p, pg_ref[...])
    backward_weights(w1_ref, wb, chans)
    out = join_planes(dot(wb[...], s_p[...], 1, 0), chans) * mask
    out_ref[...] = out.astype(BF)


def whole(shape):
    return pl.BlockSpec(shape, lambda i: (0,) * len(shape))


def call(kernel, args, specs, outs, scratch=(), cost=None):
    return pl.pallas_call(
        kernel,
        grid=(1,),
        in_specs=specs,
        out_specs=[whole(o.shape) for o in outs],
        out_shape=outs,
        scratch_shapes=list(scratch),
        compiler_params=pltpu.CompilerParams(vmem_limit_bytes=40 * 1024 * 1024),
        cost_estimate=cost,
    )(*args)


def all_sum(part, axis):
    count = lax.axis_size(axis)
    me = lax.axis_index(axis)

    def swap(x, bit):
        return lax.ppermute(x, axis, [(i, i ^ bit) for i in range(count)])

    halved, bit = [], 1
    cur = part
    while bit < count and len(halved) < 2:
        n = cur.shape[0] // 2
        upper = (me & bit) > 0
        low, high = cur[:n], cur[n:]
        cur = jnp.where(upper, high, low) + swap(jnp.where(upper, low, high).astype(BF), bit).astype(F32)
        halved.append(bit)
        bit *= 2
    while bit < count:
        sent = cur.astype(BF)
        cur = sent.astype(F32) + swap(sent, bit).astype(F32)
        bit *= 2
    cur = cur.astype(BF)
    for bit in reversed(halved):
        upper = (me & bit) > 0
        other = swap(cur, bit)
        cur = jnp.concatenate([jnp.where(upper, other, cur), jnp.where(upper, cur, other)], 0)
    return cur


def on_device(features, weight_one, weight_two, rules, cotangent):
    rows, chans = features.shape
    koff = rules.shape[1]
    ft, ct, rt = features.T, cotangent.T, rules.T
    count = lax.axis_size("slab")
    rule_spec = pl.BlockSpec((8, rows), lambda i: (1, 0))
    halo = jax.ShapeDtypeStruct((2 * chans + 16, 2 * RIM), BF)
    low, high = call(
        prep_kernel, (ft, ct, rt), [whole(ft.shape), whole(ct.shape), rule_spec], [halo, halo]
    )
    left = lax.ppermute(high, "slab", [(i, i + 1) for i in range(count - 1)])
    right = lax.ppermute(low, "slab", [(i + 1, i) for i in range(count - 1)])
    wide = rows + 4 * RIM
    pg, grads = call(
        main_kernel,
        (ft, ct, rt, left, right, weight_one, weight_two),
        [whole(ft.shape), whole(ct.shape), rule_spec, whole(left.shape), whole(right.shape),
         whole(weight_one.shape), whole(weight_two.shape)],
        [jax.ShapeDtypeStruct((chans, rows + 2 * RIM), BF),
         jax.ShapeDtypeStruct((koff * chans, 2 * chans), F32)],
        [pltpu.VMEM((9 * chans, wide), BF), pltpu.VMEM((9 * chans, wide), BF),
         pltpu.VMEM((9 * chans, 3 * chans), BF), pltpu.VMEM((3 * chans, 9 * chans), BF)],
    )
    (fg,) = call(
        last_kernel,
        (pg, rt, weight_one),
        [whole(pg.shape), rule_spec, whole(weight_one.shape)],
        [jax.ShapeDtypeStruct((chans, rows), BF)],
        [pltpu.VMEM((9 * chans, rows + 2 * RIM), BF), pltpu.VMEM((3 * chans, 9 * chans), BF)],
        pl.CostEstimate(flops=2 * rows * koff * chans * chans, bytes_accessed=2 * rows * chans * 4, transcendentals=0),
    )
    total = all_sum(grads, "slab").reshape(koff, chans, 2 * chans)
    return fg.T, total[:, :, :chans].astype(F32), total[:, :, chans:].astype(F32)


def solution(mesh):
    return jax.shard_map(
        on_device,
        mesh=mesh,
        in_specs=(
            P(("parts", "slab"), None),
            P(),
            P(),
            P(("parts", "slab"), None),
            P(("parts", "slab"), None),
        ),
        out_specs=(P(("parts", "slab"), None), P("parts", None, None), P("parts", None, None)),
        check_vma=False,
    )
```

```python
import functools

import jax
import jax.numpy as jnp
from jax import lax
from jax.experimental import pallas as pl
from jax.experimental.pallas import tpu as pltpu
from jax.sharding import PartitionSpec as P

SIDE = 16
RIM = SIDE * SIDE
BF = jnp.bfloat16
F32 = jnp.float32
OFFSETS = [dy * SIDE + dx for dy in (-1, 0, 1) for dx in (-1, 0, 1)]


def edge_masks(length):
    lane = lax.broadcasted_iota(jnp.int32, (1, length), 1)
    x, y = lane % SIDE, (lane // SIDE) % SIDE
    inside = {}
    for dy in (-1, 0, 1):
        for dx in (-1, 0, 1):
            ok = (x + dx >= 0) & (x + dx < SIDE) & (y + dy >= 0) & (y + dy < SIDE)
            inside[dy * SIDE + dx] = jnp.where(ok, 1.0, 0.0).astype(BF)
    return inside


def write_shifts(dst, values):
    length = values.shape[1]
    inside = edge_masks(length)
    chans = values.shape[0]
    for j, off in enumerate(OFFSETS):
        moved = values if off == 0 else pltpu.roll(values, (-off) % length, 1) * inside[off]
        dst[j * chans : (j + 1) * chans, :] = moved


def dot(a, b, ca, cb):
    return lax.dot_general(a, b, (((ca,), (cb,)), ((), ())), preferred_element_type=F32)


def join_planes(terms, chans):
    n = terms.shape[1]
    return (
        terms[:chans, : n - 2 * RIM]
        + terms[chans : 2 * chans, RIM : n - RIM]
        + terms[2 * chans :, 2 * RIM :]
    )


def backward_weights(w_ref, dst, chans):
    for dz in range(3):
        for j in range(9):
            dst[dz * chans : (dz + 1) * chans, j * chans : (j + 1) * chans] = w_ref[26 - (dz * 9 + j)]


def forward_weights(w_ref, dst, chans):
    for dz in range(3):
        for j in range(9):
            dst[j * chans : (j + 1) * chans, dz * chans : (dz + 1) * chans] = w_ref[dz * 9 + j]


def prep_kernel(odd_ref, f_hbm, c_hbm, r_hbm, near_ref, far_ref, f_ref, c_ref, m_ref, rules, sems):
    chans, n = f_ref.shape
    copies = [
        pltpu.make_async_copy(r_hbm.at[8:16, :], rules, sems.at[0]),
        pltpu.make_async_copy(f_hbm, f_ref, sems.at[1]),
        pltpu.make_async_copy(c_hbm, c_ref, sems.at[2]),
    ]
    for copy in copies:
        copy.start()
    copies[0].wait()
    mask = jnp.where(rules[5:6, :] >= 0, 1.0, 0.0).astype(BF)
    m_ref[...] = jnp.broadcast_to(mask, m_ref.shape)
    for copy in copies[1:]:
        copy.wait()
    f_ref[...] = f_ref[...] * mask
    c_ref[...] = c_ref[...] * mask
    odd = odd_ref[0] % 2

    def fill(ref, lanes):
        ref[:chans, :] = f_ref[:, lanes]
        ref[chans:, :] = c_ref[:, lanes]

    first, last = slice(0, RIM), slice(n - RIM, n)

    @pl.when(odd == 0)
    def _():
        fill(near_ref, last)
        fill(far_ref, first)

    @pl.when(odd != 0)
    def _():
        fill(near_ref, first)
        fill(far_ref, last)


def own_kernel(f_ref, c_ref, w1_hbm, w2_hbm, s_f, s_c, wf, wb, pre_ref, hg_ref, w1, w2, sems):
    chans, n = f_ref.shape
    copies = [
        pltpu.make_async_copy(w1_hbm, w1, sems.at[0]),
        pltpu.make_async_copy(w2_hbm, w2, sems.at[1]),
    ]
    for copy in copies:
        copy.start()
    write_shifts(s_f, f_ref[...])
    write_shifts(s_c, c_ref[...])
    copies[0].wait()
    forward_weights(w1, wf, chans)
    spread_terms(pre_ref, dot(wf[...], s_f[...], 0, 0), chans)
    copies[1].wait()
    backward_weights(w2, wb, chans)
    spread_terms(hg_ref, dot(wb[...], s_c[...], 1, 0), chans)


def spread_terms(out_ref, terms, chans):
    n = terms.shape[1]
    low, mid, high = terms[:chans], terms[chans : 2 * chans], terms[2 * chans :]
    out_ref[:, :RIM] = high[:, :RIM]
    out_ref[:, RIM : 2 * RIM] = mid[:, :RIM] + high[:, RIM : 2 * RIM]
    out_ref[:, 2 * RIM : n] = mid[:, RIM : n - RIM] + high[:, 2 * RIM :] + low[:, : n - 2 * RIM]
    out_ref[:, n : n + RIM] = mid[:, n - RIM :] + low[:, n - 2 * RIM : n - RIM]
    out_ref[:, n + RIM :] = low[:, n - RIM :]


def sides(odd_ref, near, far):
    far = jnp.where(odd_ref[0] >= 2, far, jnp.zeros_like(far))
    even = odd_ref[0] % 2 == 0
    return jnp.where(even, far, near), jnp.where(even, near, far)


def slope(hg, pre, mask):
    sig = 1.0 / (1.0 + jnp.exp(-pre))
    return pre * sig * mask, (hg * mask * sig * (1.0 + pre * (1.0 - sig))).astype(BF)


def grads_kernel(odd_ref, far_ref, near_ref, m_ref, s_f, s_c, wf, wb, pre_ref, hg_ref,
                 keep_ref, send_ref, far_pg_ref, pg_ref, r_f, r_c, grads_ref):
    chans = pg_ref.shape[0]
    n = s_f.shape[1]
    both = jnp.concatenate(sides(odd_ref, near_ref[...], far_ref[...]), 1)
    write_shifts(r_f, both[:chans, :])
    write_shifts(r_c, both[chans:, :])
    rim = slice(0, RIM)
    end = slice(RIM, 2 * RIM)
    low_pre = dot(wf[:, :chans], r_f[:, rim], 0, 0)
    high_pre = dot(wf[:, 2 * chans :], r_f[:, end], 0, 0)
    low_hg = dot(wb[:chans, :], r_c[:, rim], 1, 0)
    high_hg = dot(wb[2 * chans :, :], r_c[:, end], 1, 0)
    mask = m_ref[0:1, :].astype(F32)

    def own(ref, low, high):
        mid = ref[:, RIM : RIM + n]
        return jnp.concatenate([mid[:, :RIM] + low, mid[:, RIM : n - RIM], mid[:, n - RIM :] + high], 1)

    hidden, pg = slope(own(hg_ref, low_hg, high_hg), own(pre_ref, low_pre, high_pre), mask)
    pg_ref[...] = pg
    hidden = hidden.astype(BF)
    blank = jnp.zeros((chans, RIM), BF)

    def fan(v):
        return jnp.concatenate(
            [jnp.concatenate([v[:, RIM:], blank], 1), v, jnp.concatenate([blank, v[:, : n - RIM]], 1)], 0
        )

    g1 = dot(s_f[...], fan(pg), 1, 1)
    g1_low = dot(r_f[:, rim], pg[:, :RIM], 1, 1)
    g1_high = dot(r_f[:, end], pg[:, n - RIM :], 1, 1)
    g2 = dot(fan(hidden), s_c[...], 1, 1)
    g2_low = dot(hidden[:, :RIM], r_c[:, rim], 1, 1)
    g2_high = dot(hidden[:, n - RIM :], r_c[:, end], 1, 1)
    for dz in range(3):
        for j in range(9):
            k = dz * 9 + j
            bz, bj = 2 - dz, 8 - j
            rows = slice(j * chans, (j + 1) * chans)
            one = g1[rows, dz * chans : (dz + 1) * chans]
            cols = slice(bj * chans, (bj + 1) * chans)
            two = g2[bz * chans : (bz + 1) * chans, cols]
            if dz == 0:
                one = one + g1_low[rows, :]
                two = two + g2_high[:, cols]
            if dz == 2:
                one = one + g1_high[rows, :]
                two = two + g2_low[:, cols]
            grads_ref[k * chans : (k + 1) * chans, :chans] = one
            grads_ref[k * chans : (k + 1) * chans, chans:] = two


    half = keep_ref.shape[0]

    def part_with(mine, yours, near_plane, far_plane):
        keep_ref[...] = grads_ref[mine, :]
        send_ref[:half, :] = grads_ref[yours, :].astype(BF)
        for i in range(RIM // (2 * chans)):
            lanes = slice(near_plane + 2 * i * chans, near_plane + 2 * (i + 1) * chans)
            send_ref[half + i * chans : half + (i + 1) * chans, :] = pg[:, lanes]
        far_pg_ref[...] = pg[:, far_plane : far_plane + RIM]

    lower, upper = slice(0, half), slice(half, 2 * half)

    @pl.when(odd_ref[0] % 2 == 0)
    def _():
        part_with(lower, upper, n - RIM, 0)

    @pl.when(odd_ref[0] % 2 != 0)
    def _():
        part_with(upper, lower, 0, n - RIM)


def last_kernel(odd_ref, near_ref, far_ref, m_ref, pg_ref, w1_hbm, _, out_ref, zero_ref, s_p, wb, w1, sems):
    chans, n = pg_ref.shape
    weights = pltpu.make_async_copy(w1_hbm, w1, sems.at[0])
    weights.start()
    zero_ref[...] = jnp.zeros_like(zero_ref)
    first = near_ref.shape[0] - RIM // 2
    near = jnp.concatenate(
        [near_ref[first + i * chans : first + (i + 1) * chans, :] for i in range(RIM // (2 * chans))], 1
    )
    left, right = sides(odd_ref, near, far_ref[...])
    write_shifts(s_p, jnp.concatenate([left, pg_ref[...], right], 1))
    weights.wait()
    backward_weights(w1, wb, chans)
    out = join_planes(dot(wb[...], s_p[...], 1, 0), chans) * m_ref[0:1, :].astype(F32)
    out_ref[...] = out.astype(BF)


def whole(shape):
    return pl.BlockSpec(shape, lambda i: (0,) * len(shape))


HBM = pl.BlockSpec(memory_space=pltpu.HBM)
SCALAR = pl.BlockSpec(memory_space=pltpu.SMEM)


def call(kernel, args, outs, scratch=(), specs=None, flops=0):
    specs = specs or {}
    args = [
        pltpu.with_memory_space_constraint(x, pltpu.HBM) if specs.get(i) is HBM else x
        for i, x in enumerate(args)
    ]
    return pl.pallas_call(
        kernel,
        grid=(1,),
        in_specs=[specs.get(i, whole(x.shape)) for i, x in enumerate(args)],
        out_specs=[whole(o.shape) for o in outs],
        out_shape=outs,
        scratch_shapes=list(scratch),
        compiler_params=pltpu.CompilerParams(vmem_limit_bytes=40 * 1024 * 1024),
        cost_estimate=pl.CostEstimate(flops=flops, bytes_accessed=0, transcendentals=0) if flops else None,
    )(*args)


def all_sum(keep, send, axis, beside):
    count = lax.axis_size(axis)
    me = lax.axis_index(axis)

    def swap(x, bit):
        return lax.ppermute(x, axis, [(i, i ^ bit) for i in range(count)])

    came = swap(send, 1)
    cur = keep + came[: keep.shape[0]].astype(F32)
    halved, bit = [1], 2
    while bit < count and len(halved) < 2:
        n = cur.shape[0] // 2
        upper = (me & bit) > 0
        low, high = cur[:n], cur[n:]
        cur = jnp.where(upper, high, low) + swap(jnp.where(upper, low, high).astype(BF), bit).astype(F32)
        halved.append(bit)
        bit *= 2
    zero = None
    while bit < count:
        sent = cur.astype(BF)
        other = swap(sent, bit)
        bit *= 2
        if bit >= count:
            zero = beside(came, sent)
        cur = sent.astype(F32) + other.astype(F32)
    if zero is None:
        zero = beside(came, cur.astype(BF))
    cur = (cur + zero).astype(BF)
    for bit in reversed(halved):
        upper = (me & bit) > 0
        other = swap(cur, bit)
        cur = jnp.concatenate([jnp.where(upper, other, cur), jnp.where(upper, cur, other)], 0)
    return cur


def far_partners(parts, count):
    pairs = []
    for part in range(parts):
        base = part * count
        for i in range(1, count - 1, 2):
            pairs += [(base + i, base + i + 1), (base + i + 1, base + i)]
        other = part ^ 1
        if other < parts:
            pairs += [(base, other * count), (base + count - 1, other * count + count - 1)]
    return pairs


def on_device(features, weight_one, weight_two, rules, cotangent):
    rows, chans = features.shape
    koff = rules.shape[1]
    ft, ct, rt = features.T, cotangent.T, rules.T
    count = lax.axis_size("slab")
    me = lax.axis_index("slab")
    inner = (me > 0) & (me < count - 1)
    odd = (me % 2 + 2 * inner.astype(me.dtype)).astype(jnp.int32).reshape(1)

    def array(*shape, kind=BF):
        return jax.ShapeDtypeStruct(shape, kind)

    def dma(n):
        return pltpu.SemaphoreType.DMA((n,))

    halo = (2 * chans, RIM)
    taps = 9 * chans
    weights = pltpu.VMEM(weight_one.shape, BF)
    near, far, f, c, m = call(
        prep_kernel,
        (odd, ft, ct, rt),
        [array(*halo), array(*halo), array(chans, rows), array(chans, rows), array(16, rows)],
        [pltpu.VMEM((8, rows), jnp.int32), dma(3)],
        {0: SCALAR, 1: HBM, 2: HBM, 3: HBM},
    )
    far_pairs = far_partners(lax.axis_size("parts"), count)
    near_pairs = [(i, i ^ 1) for i in range(count)]
    near_in = lax.ppermute(near, "slab", near_pairs)
    far_in = lax.ppermute(far, ("parts", "slab"), far_pairs)
    s_f, s_c, wf, wb, pre, hg = call(
        own_kernel,
        (f, c, weight_one, weight_two),
        [array(taps, rows), array(taps, rows), array(taps, 3 * chans), array(3 * chans, taps),
         array(chans, rows + 2 * RIM, kind=F32), array(chans, rows + 2 * RIM, kind=F32)],
        [weights, weights, dma(2)],
        {2: HBM, 3: HBM},
        flops=2 * 2 * rows * koff * chans * chans,
    )
    half = koff * chans // 2
    keep, send, far_pg, pg = call(
        grads_kernel,
        (odd, far_in, near_in, m, s_f, s_c, wf, wb, pre, hg),
        [array(half, 2 * chans, kind=F32), array(half + RIM // 2, 2 * chans), array(chans, RIM), array(chans, rows)],
        [pltpu.VMEM((taps, 2 * RIM), BF), pltpu.VMEM((taps, 2 * RIM), BF), pltpu.VMEM((2 * half, 2 * chans), F32)],
        {0: SCALAR},
        flops=2 * 2 * rows * koff * chans * chans,
    )
    far_pg = lax.ppermute(far_pg, ("parts", "slab"), far_pairs)
    done = []

    def beside(came, sent):
        fg, zero = call(
            last_kernel,
            (odd, came, far_pg, m, pg, weight_one, sent),
            [array(chans, rows), array(8, 2 * chans, kind=F32)],
            [pltpu.VMEM((taps, rows + 2 * RIM), BF), pltpu.VMEM((3 * chans, taps), BF), weights, dma(1)],
            {0: SCALAR, 5: HBM, 6: pl.BlockSpec(memory_space=pl.ANY)},
            flops=2 * 2 * rows * koff * chans * chans,
        )
        done.append(fg)
        return zero[:1]

    total = all_sum(keep, send, "slab", beside).reshape(koff, chans, 2 * chans)
    return done[0].T, total[:, :, :chans].astype(F32), total[:, :, chans:].astype(F32)


def solution(mesh):
    return jax.shard_map(
        on_device,
        mesh=mesh,
        in_specs=(
            P(("parts", "slab"), None),
            P(),
            P(),
            P(("parts", "slab"), None),
            P(("parts", "slab"), None),
        ),
        out_specs=(P(("parts", "slab"), None), P("parts", None, None), P("parts", None, None)),
        check_vma=False,
    )
```

```python
import functools

import jax
import jax.numpy as jnp
from jax import lax
from jax.experimental import pallas as pl
from jax.experimental.pallas import tpu as pltpu
from jax.sharding import PartitionSpec as P

SIDE = 16
RIM = SIDE * SIDE
BF = jnp.bfloat16
F32 = jnp.float32
OFFSETS = [dy * SIDE + dx for dy in (-1, 0, 1) for dx in (-1, 0, 1)]


def edge_masks(length):
    lane = lax.broadcasted_iota(jnp.int32, (1, length), 1)
    x, y = lane % SIDE, (lane // SIDE) % SIDE
    inside = {}
    for dy in (-1, 0, 1):
        for dx in (-1, 0, 1):
            ok = (x + dx >= 0) & (x + dx < SIDE) & (y + dy >= 0) & (y + dy < SIDE)
            inside[dy * SIDE + dx] = jnp.where(ok, 1.0, 0.0).astype(BF)
    return inside


def write_shifts(dst, values):
    length = values.shape[1]
    inside = edge_masks(length)
    chans = values.shape[0]
    for j, off in enumerate(OFFSETS):
        moved = values if off == 0 else pltpu.roll(values, (-off) % length, 1) * inside[off]
        dst[j * chans : (j + 1) * chans, :] = moved


def dot(a, b, ca, cb):
    return lax.dot_general(a, b, (((ca,), (cb,)), ((), ())), preferred_element_type=F32)


def join_planes(terms, chans):
    n = terms.shape[1]
    return (
        terms[:chans, : n - 2 * RIM]
        + terms[chans : 2 * chans, RIM : n - RIM]
        + terms[2 * chans :, 2 * RIM :]
    )


def backward_weights(w_ref, dst, chans):
    for dz in range(3):
        for j in range(9):
            dst[dz * chans : (dz + 1) * chans, j * chans : (j + 1) * chans] = w_ref[26 - (dz * 9 + j)]


def forward_weights(w_ref, dst, chans):
    for dz in range(3):
        for j in range(9):
            dst[j * chans : (j + 1) * chans, dz * chans : (dz + 1) * chans] = w_ref[dz * 9 + j]


def prep_kernel(odd_ref, f_hbm, c_hbm, r_hbm, near_ref, far_ref, f_ref, c_ref, m_ref, rules, sems):
    chans, n = f_ref.shape
    copies = [
        pltpu.make_async_copy(r_hbm.at[8:16, :], rules, sems.at[0]),
        pltpu.make_async_copy(f_hbm, f_ref, sems.at[1]),
        pltpu.make_async_copy(c_hbm, c_ref, sems.at[2]),
    ]
    for copy in copies:
        copy.start()
    copies[0].wait()
    mask = jnp.where(rules[5:6, :] >= 0, 1.0, 0.0).astype(BF)
    m_ref[...] = jnp.broadcast_to(mask, m_ref.shape)
    for copy in copies[1:]:
        copy.wait()
    f_ref[...] = f_ref[...] * mask
    c_ref[...] = c_ref[...] * mask
    odd = odd_ref[0] % 2

    def fill(ref, lanes):
        ref[:chans, :] = f_ref[:, lanes]
        ref[chans:, :] = c_ref[:, lanes]

    first, last = slice(0, RIM), slice(n - RIM, n)

    @pl.when(odd == 0)
    def _():
        fill(near_ref, last)
        fill(far_ref, first)

    @pl.when(odd != 0)
    def _():
        fill(near_ref, first)
        fill(far_ref, last)


def own_kernel(f_ref, c_ref, w1_hbm, w2_hbm, s_f, s_c, wf, wb, pre_ref, hg_ref, w1, w2, turned, sems):
    chans, n = f_ref.shape
    copies = [
        pltpu.make_async_copy(w1_hbm, w1, sems.at[0]),
        pltpu.make_async_copy(w2_hbm, w2, sems.at[1]),
    ]
    for copy in copies:
        copy.start()
    for copy in copies:
        copy.wait()
    write_shifts(s_f, f_ref[...])
    write_shifts(s_c, c_ref[...])
    forward_weights(w1, turned, chans)
    wf[...] = turned[...].T
    spread_terms(pre_ref, dot(wf[...], s_f[...], 1, 0), chans)
    backward_weights(w2, wb, chans)
    spread_terms(hg_ref, dot(wb[...], s_c[...], 1, 0), chans)


def spread_terms(out_ref, terms, chans):
    n = terms.shape[1]
    low, mid, high = terms[:chans], terms[chans : 2 * chans], terms[2 * chans :]
    out_ref[:, :RIM] = high[:, :RIM]
    out_ref[:, RIM : 2 * RIM] = mid[:, :RIM] + high[:, RIM : 2 * RIM]
    out_ref[:, 2 * RIM : n] = mid[:, RIM : n - RIM] + high[:, 2 * RIM :] + low[:, : n - 2 * RIM]
    out_ref[:, n : n + RIM] = mid[:, n - RIM :] + low[:, n - 2 * RIM : n - RIM]
    out_ref[:, n + RIM :] = low[:, n - RIM :]


def sides(odd_ref, near, far):
    far = jnp.where(odd_ref[0] >= 2, far, jnp.zeros_like(far))
    even = odd_ref[0] % 2 == 0
    return jnp.where(even, far, near), jnp.where(even, near, far)


def slope(hg, pre, mask):
    sig = 1.0 / (1.0 + jnp.exp(-pre))
    return pre * sig * mask, (hg * mask * sig * (1.0 + pre * (1.0 - sig))).astype(BF)


def grads_kernel(odd_ref, far_ref, near_ref, m_ref, s_f, s_c, wf, wb, pre_ref, hg_ref,
                 keep_ref, send_ref, far_pg_ref, pg_ref, r_f, r_c, one_ref, two_ref):
    chans = pg_ref.shape[0]
    n = s_f.shape[1]
    both = jnp.concatenate(sides(odd_ref, near_ref[...], far_ref[...]), 1)
    write_shifts(r_f, both[:chans, :])
    write_shifts(r_c, both[chans:, :])
    rim = slice(0, RIM)
    end = slice(RIM, 2 * RIM)
    low_pre = dot(wf[:chans, :], r_f[:, rim], 1, 0)
    high_pre = dot(wf[2 * chans :, :], r_f[:, end], 1, 0)
    low_hg = dot(wb[:chans, :], r_c[:, rim], 1, 0)
    high_hg = dot(wb[2 * chans :, :], r_c[:, end], 1, 0)
    mask = m_ref[0:1, :].astype(F32)

    def own(ref, low, high):
        mid = ref[:, RIM : RIM + n]
        return jnp.concatenate([mid[:, :RIM] + low, mid[:, RIM : n - RIM], mid[:, n - RIM :] + high], 1)

    hidden, pg = slope(own(hg_ref, low_hg, high_hg), own(pre_ref, low_pre, high_pre), mask)
    pg_ref[...] = pg
    hidden = hidden.astype(BF)
    blank = jnp.zeros((chans, RIM), BF)

    def fan(v):
        return jnp.concatenate(
            [jnp.concatenate([v[:, RIM:], blank], 1), v, jnp.concatenate([blank, v[:, : n - RIM]], 1)], 0
        )

    def rim_fan(v, low, high):
        parts = [jnp.concatenate([v[:, :RIM], blank], 1), jnp.concatenate([blank, v[:, n - RIM :]], 1)]
        none = jnp.zeros((chans, 2 * RIM), BF)
        return jnp.concatenate([parts[low], none, parts[high]], 0)

    one_ref[...] = dot(s_f[...], fan(pg), 1, 1) + dot(r_f[...], rim_fan(pg, 0, 1), 1, 1)
    two_ref[...] = dot(fan(hidden), s_c[...], 1, 1) + dot(rim_fan(hidden, 0, 1), r_c[...], 1, 1)
    half = keep_ref.shape[0]

    def part_with(pack_mine, pack_yours, near_plane, far_plane):
        pack_mine(keep_ref)
        pack_yours(send_ref)
        for i in range(RIM // (2 * chans)):
            lanes = slice(near_plane + 2 * i * chans, near_plane + 2 * (i + 1) * chans)
            send_ref[half + i * chans : half + (i + 1) * chans, :] = pg[:, lanes]
        far_pg_ref[...] = pg[:, far_plane : far_plane + RIM]

    @pl.when(odd_ref[0] % 2 == 0)
    def _():
        part_with(lambda ref: pack_one(ref, one_ref), lambda ref: pack_two(ref, two_ref), n - RIM, 0)

    @pl.when(odd_ref[0] % 2 != 0)
    def _():
        part_with(lambda ref: pack_two(ref, two_ref), lambda ref: pack_one(ref, one_ref), 0, n - RIM)


def pack_one(ref, one_ref):
    taps, chans = one_ref.shape[0], one_ref.shape[1] // 3
    fold = taps // 2
    ref[:taps, :] = one_ref[:, : 2 * chans].astype(ref.dtype)
    last = one_ref[:, 2 * chans :].astype(ref.dtype)
    ref[taps : taps + fold, :chans] = last[:fold]
    ref[taps : taps + fold, chans:] = last[fold:]


def pack_two(ref, two_ref):
    deep, chans = two_ref.shape[0], two_ref.shape[0] // 3
    fold = deep // 2
    for t in range(4):
        ref[t * deep : (t + 1) * deep, :] = two_ref[:, 2 * t * chans : 2 * (t + 1) * chans].astype(ref.dtype)
    last = two_ref[:, 8 * chans :].astype(ref.dtype)
    ref[4 * deep : 4 * deep + fold, :chans] = last[:fold]
    ref[4 * deep : 4 * deep + fold, chans:] = last[fold:]


def unpack_one(src, dst, dz):
    chans = dst.shape[1]
    taps = 9 * chans
    fold = taps // 2
    for j in range(9):
        first, k = j * chans, dz * 9 + j
        if dz < 2:
            dst[k] = src[first : first + chans, dz * chans : (dz + 1) * chans].astype(F32)
            continue
        for begin in range(first, first + chans, chans // 2):
            row, lane = taps + begin % fold, begin // fold * chans
            at = begin - first
            dst[k, at : at + chans // 2, :] = src[row : row + chans // 2, lane : lane + chans].astype(F32)


def unpack_two(src, dst, dz):
    chans = dst.shape[1]
    deep = 3 * chans
    fold = deep // 2
    first = (2 - dz) * chans
    for j in range(9):
        mirror, k = 8 - j, dz * 9 + j
        if mirror < 8:
            row, lane = mirror // 2 * deep + first, mirror % 2 * chans
            dst[k] = src[row : row + chans, lane : lane + chans].astype(F32)
            continue
        for begin in range(first, first + chans, chans // 2):
            row, lane = 4 * deep + begin % fold, begin // fold * chans
            at = begin - first
            dst[k, at : at + chans // 2, :] = src[row : row + chans // 2, lane : lane + chans].astype(F32)


def write_half(src, one_hbm, two_hbm, wide, sems, is_one):
    def write(unpack, out):
        copies = []
        for dz in range(3):
            unpack(src, wide, dz)
            third = pl.ds(dz * 9, 9)
            copies.append(pltpu.make_async_copy(wide.at[third], out.at[third], sems.at[dz]))
            copies[-1].start()
        for copy in copies:
            copy.wait()

    @pl.when(is_one)
    def _():
        write(unpack_one, one_hbm)

    @pl.when(jnp.logical_not(is_one))
    def _():
        write(unpack_two, two_hbm)


def mine_kernel(odd_ref, src, one_hbm, two_hbm, wide, sems):
    write_half(src, one_hbm, two_hbm, wide, sems, odd_ref[0] % 2 == 0)


def yours_kernel(odd_ref, src, _one, _two, one_hbm, two_hbm, wide, sems):
    write_half(src, one_hbm, two_hbm, wide, sems, odd_ref[0] % 2 != 0)


def last_kernel(odd_ref, near_ref, far_ref, m_ref, pg_ref, w1_hbm, _, out_ref, zero_ref, s_p, wb, w1, sems):
    chans, n = pg_ref.shape
    weights = pltpu.make_async_copy(w1_hbm, w1, sems.at[0])
    weights.start()
    zero_ref[...] = jnp.zeros_like(zero_ref)
    first = near_ref.shape[0] - RIM // 2
    near = jnp.concatenate(
        [near_ref[first + i * chans : first + (i + 1) * chans, :] for i in range(RIM // (2 * chans))], 1
    )
    left, right = sides(odd_ref, near, far_ref[...])
    write_shifts(s_p, jnp.concatenate([left, pg_ref[...], right], 1))
    weights.wait()
    backward_weights(w1, wb, chans)
    out = join_planes(dot(wb[...], s_p[...], 1, 0), chans) * m_ref[0:1, :].astype(F32)
    out_ref[...] = out.astype(BF)


def whole(shape):
    return pl.BlockSpec(shape, lambda i: (0,) * len(shape))


HBM = pl.BlockSpec(memory_space=pltpu.HBM)
ANY = pl.BlockSpec(memory_space=pl.ANY)
SCALAR = pl.BlockSpec(memory_space=pltpu.SMEM)


def call(kernel, args, outs, scratch=(), specs=None, flops=0, out_specs=None, aliases=None):
    specs = specs or {}
    args = [
        pltpu.with_memory_space_constraint(x, pltpu.HBM) if specs.get(i) is HBM else x
        for i, x in enumerate(args)
    ]
    return pl.pallas_call(
        kernel,
        grid=(1,),
        in_specs=[specs.get(i, whole(x.shape)) for i, x in enumerate(args)],
        out_specs=out_specs or [whole(o.shape) for o in outs],
        input_output_aliases=aliases or {},
        out_shape=outs,
        scratch_shapes=list(scratch),
        compiler_params=pltpu.CompilerParams(vmem_limit_bytes=40 * 1024 * 1024),
        cost_estimate=pl.CostEstimate(flops=flops, bytes_accessed=0, transcendentals=0) if flops else None,
    )(*args)


def all_sum(keep, send, axis, beside):
    count = lax.axis_size(axis)
    me = lax.axis_index(axis)
    is_odd = (me & 1) > 0
    bits = [1 << i for i in range(1, count.bit_length() - 1)]
    even_bits, odd_bits = bits, bits[1:] + bits[:1]

    def swap(x, step):
        bit = (even_bits[step], odd_bits[step])
        return lax.ppermute(x, axis, [(i, i ^ bit[i & 1]) for i in range(count)])

    def neighbour(x):
        return lax.ppermute(x, axis, [(i, i ^ 1) for i in range(count)])

    came = neighbour(send)
    cur = keep + came[: keep.shape[0]].astype(F32)
    upper = (me & jnp.where(is_odd, odd_bits[0], even_bits[0])) > 0
    n = cur.shape[0] // 2
    low, high = cur[:n], cur[n:]
    cur = jnp.where(upper, high, low) + swap(jnp.where(upper, low, high).astype(BF), 0).astype(F32)
    for step in range(1, len(bits)):
        sent = cur.astype(BF)
        other = swap(sent, step)
        if step == len(bits) - 1:
            zero = beside(came, sent)
        cur = sent.astype(F32) + other.astype(F32)
    cur = (cur + zero).astype(BF)
    other = swap(cur, 0)
    cur = jnp.concatenate([jnp.where(upper, other, cur), jnp.where(upper, cur, other)], 0)
    return cur, neighbour(cur)


def far_partners(parts, count):
    pairs = []
    for part in range(parts):
        base = part * count
        for i in range(1, count - 1, 2):
            pairs += [(base + i, base + i + 1), (base + i + 1, base + i)]
        other = part ^ 1
        if other < parts:
            pairs += [(base, other * count), (base + count - 1, other * count + count - 1)]
    return pairs


def on_device(features, weight_one, weight_two, rules, cotangent):
    rows, chans = features.shape
    koff = rules.shape[1]
    ft, ct, rt = features.T, cotangent.T, rules.T
    count = lax.axis_size("slab")
    me = lax.axis_index("slab")
    inner = (me > 0) & (me < count - 1)
    odd = (me % 2 + 2 * inner.astype(me.dtype)).astype(jnp.int32).reshape(1)

    def array(*shape, kind=BF):
        return jax.ShapeDtypeStruct(shape, kind)

    def dma(n):
        return pltpu.SemaphoreType.DMA((n,))

    halo = (2 * chans, RIM)
    taps = 9 * chans
    weights = pltpu.VMEM(weight_one.shape, BF)
    near, far, f, c, m = call(
        prep_kernel,
        (odd, ft, ct, rt),
        [array(*halo), array(*halo), array(chans, rows), array(chans, rows), array(16, rows)],
        [pltpu.VMEM((8, rows), jnp.int32), dma(3)],
        {0: SCALAR, 1: HBM, 2: HBM, 3: HBM},
    )
    far_pairs = far_partners(lax.axis_size("parts"), count)
    near_pairs = [(i, i ^ 1) for i in range(count)]
    near_in = lax.ppermute(near, "slab", near_pairs)
    far_in = lax.ppermute(far, ("parts", "slab"), far_pairs)
    s_f, s_c, wf, wb, pre, hg = call(
        own_kernel,
        (f, c, weight_one, weight_two),
        [array(taps, rows), array(taps, rows), array(3 * chans, taps), array(3 * chans, taps),
         array(chans, rows + 2 * RIM, kind=F32), array(chans, rows + 2 * RIM, kind=F32)],
        [weights, weights, pltpu.VMEM((taps, 3 * chans), BF), dma(2)],
        {2: HBM, 3: HBM},
        flops=2 * 2 * rows * koff * chans * chans,
    )
    half = koff * chans // 2
    keep, send, far_pg, pg = call(
        grads_kernel,
        (odd, far_in, near_in, m, s_f, s_c, wf, wb, pre, hg),
        [array(half, 2 * chans, kind=F32), array(half + RIM // 2, 2 * chans), array(chans, RIM), array(chans, rows)],
        [pltpu.VMEM((taps, 2 * RIM), BF), pltpu.VMEM((taps, 2 * RIM), BF), pltpu.VMEM((taps, 3 * chans), F32), pltpu.VMEM((3 * chans, taps), F32)],
        {0: SCALAR},
        flops=2 * 2 * rows * koff * chans * chans,
    )
    far_pg = lax.ppermute(far_pg, ("parts", "slab"), far_pairs)
    done = []

    def beside(came, sent):
        fg, zero = call(
            last_kernel,
            (odd, came, far_pg, m, pg, weight_one, sent),
            [array(chans, rows), array(8, 2 * chans, kind=F32)],
            [pltpu.VMEM((taps, rows + 2 * RIM), BF), pltpu.VMEM((3 * chans, taps), BF), weights, dma(1)],
            {0: SCALAR, 5: HBM, 6: ANY},
            flops=2 * 2 * rows * koff * chans * chans,
        )
        done.append(fg)
        return zero[:1]

    mine, yours = all_sum(keep, send, "slab", beside)
    grads = [array(koff, chans, chans, kind=F32)] * 2
    scratch = [pltpu.VMEM((koff, chans, chans), F32), dma(3)]
    grads_out = call(
        mine_kernel, (odd, mine), grads, scratch, {0: SCALAR}, flops=2 * rows * koff * chans * chans,
        out_specs=[ANY, ANY],
    )
    grad_one, grad_two = call(
        yours_kernel, (odd, yours, *grads_out), grads, scratch, {0: SCALAR, 2: ANY, 3: ANY},
        out_specs=[ANY, ANY], aliases={2: 0, 3: 1},
    )
    return done[0].T, grad_one, grad_two


def solution(mesh):
    return jax.shard_map(
        on_device,
        mesh=mesh,
        in_specs=(
            P(("parts", "slab"), None),
            P(),
            P(),
            P(("parts", "slab"), None),
            P(("parts", "slab"), None),
        ),
        out_specs=(P(("parts", "slab"), None), P("parts", None, None), P("parts", None, None)),
        check_vma=False,
    )
```

```python
import functools

import jax
import jax.numpy as jnp
from jax import lax
from jax.experimental import pallas as pl
from jax.experimental.pallas import tpu as pltpu
from jax.sharding import PartitionSpec as P

SIDE = 16
RIM = SIDE * SIDE
BF = jnp.bfloat16
F32 = jnp.float32
OFFSETS = [dy * SIDE + dx for dy in (-1, 0, 1) for dx in (-1, 0, 1)]


def edge_masks(length):
    lane = lax.broadcasted_iota(jnp.int32, (1, length), 1)
    x, y = lane % SIDE, (lane // SIDE) % SIDE
    inside = {}
    for dy in (-1, 0, 1):
        for dx in (-1, 0, 1):
            ok = (x + dx >= 0) & (x + dx < SIDE) & (y + dy >= 0) & (y + dy < SIDE)
            inside[dy * SIDE + dx] = jnp.where(ok, 1.0, 0.0).astype(BF)
    return inside


def write_shifts(dst, values):
    length = values.shape[1]
    inside = edge_masks(length)
    chans = values.shape[0]
    for j, off in enumerate(OFFSETS):
        moved = values if off == 0 else pltpu.roll(values, (-off) % length, 1) * inside[off]
        dst[j * chans : (j + 1) * chans, :] = moved


def dot(a, b, ca, cb):
    return lax.dot_general(a, b, (((ca,), (cb,)), ((), ())), preferred_element_type=F32)


def join_planes(terms, chans):
    n = terms.shape[1]
    return (
        terms[:chans, : n - 2 * RIM]
        + terms[chans : 2 * chans, RIM : n - RIM]
        + terms[2 * chans :, 2 * RIM :]
    )


def backward_weights(w_ref, dst, chans):
    for dz in range(3):
        for j in range(9):
            dst[dz * chans : (dz + 1) * chans, j * chans : (j + 1) * chans] = w_ref[26 - (dz * 9 + j)]


def forward_weights(w_ref, dst, chans):
    for dz in range(3):
        for j in range(9):
            dst[j * chans : (j + 1) * chans, dz * chans : (dz + 1) * chans] = w_ref[dz * 9 + j]


def prep_kernel(odd_ref, f_hbm, c_hbm, r_hbm, near_ref, far_ref, f_ref, c_ref, m_ref, rules, sems):
    chans, n = f_ref.shape
    copies = [
        pltpu.make_async_copy(r_hbm.at[8:16, :], rules, sems.at[0]),
        pltpu.make_async_copy(f_hbm, f_ref, sems.at[1]),
        pltpu.make_async_copy(c_hbm, c_ref, sems.at[2]),
    ]
    for copy in copies:
        copy.start()
    copies[0].wait()
    mask = jnp.where(rules[5:6, :] >= 0, 1.0, 0.0).astype(BF)
    m_ref[...] = jnp.broadcast_to(mask, m_ref.shape)
    for copy in copies[1:]:
        copy.wait()
    f_ref[...] = f_ref[...] * mask
    c_ref[...] = c_ref[...] * mask
    odd = odd_ref[0] % 2

    def fill(ref, lanes):
        ref[:chans, :] = f_ref[:, lanes]
        ref[chans:, :] = c_ref[:, lanes]

    first, last = slice(0, RIM), slice(n - RIM, n)

    @pl.when(odd == 0)
    def _():
        fill(near_ref, last)
        fill(far_ref, first)

    @pl.when(odd != 0)
    def _():
        fill(near_ref, first)
        fill(far_ref, last)


def own_kernel(odd_ref, f_ref, c_ref, w1_hbm, w2_hbm, s_keep, s_send, wf, wb, pre_ref, hg_ref, w1, w2, turned, sems):
    chans, n = f_ref.shape
    copies = [
        pltpu.make_async_copy(w1_hbm, w1, sems.at[0]),
        pltpu.make_async_copy(w2_hbm, w2, sems.at[1]),
    ]
    for copy in copies:
        copy.start()
    for copy in copies:
        copy.wait()

    def work(s_f, s_c):
        write_shifts(s_f, f_ref[...])
        write_shifts(s_c, c_ref[...])
        forward_weights(w1, turned, chans)
        wf[...] = turned[...].T
        spread_terms(pre_ref, dot(wf[...], s_f[...], 1, 0), chans)
        backward_weights(w2, wb, chans)
        spread_terms(hg_ref, dot(wb[...], s_c[...], 1, 0), chans)

    @pl.when(odd_ref[0] % 2 == 0)
    def _():
        work(s_keep, s_send)

    @pl.when(odd_ref[0] % 2 != 0)
    def _():
        work(s_send, s_keep)


def spread_terms(out_ref, terms, chans):
    n = terms.shape[1]
    low, mid, high = terms[:chans], terms[chans : 2 * chans], terms[2 * chans :]
    out_ref[:, :RIM] = high[:, :RIM]
    out_ref[:, RIM : 2 * RIM] = mid[:, :RIM] + high[:, RIM : 2 * RIM]
    out_ref[:, 2 * RIM : n] = mid[:, RIM : n - RIM] + high[:, 2 * RIM :] + low[:, : n - 2 * RIM]
    out_ref[:, n : n + RIM] = mid[:, n - RIM :] + low[:, n - 2 * RIM : n - RIM]
    out_ref[:, n + RIM :] = low[:, n - RIM :]


def sides(odd_ref, near, far):
    far = jnp.where(odd_ref[0] >= 2, far, jnp.zeros_like(far))
    even = odd_ref[0] % 2 == 0
    return jnp.where(even, far, near), jnp.where(even, near, far)


def slope(hg, pre, mask):
    sig = 1.0 / (1.0 + jnp.exp(-pre))
    return pre * sig * mask, (hg * mask * sig * (1.0 + pre * (1.0 - sig))).astype(BF)


def fan(v):
    blank = jnp.zeros((v.shape[0], RIM), BF)
    after = jnp.concatenate([v[:, RIM:], blank], 1)
    before = jnp.concatenate([blank, v[:, : v.shape[1] - RIM]], 1)
    return jnp.concatenate([after, v, before], 0)


def rim_fan(v):
    blank = jnp.zeros((v.shape[0], RIM), BF)
    first = jnp.concatenate([v[:, :RIM], blank], 1)
    last = jnp.concatenate([blank, v[:, v.shape[1] - RIM :]], 1)
    return jnp.concatenate([first, jnp.zeros_like(first), last], 0)


def grad_one(ref, s_f, r_f, pg, one_ref):
    one_ref[...] = dot(s_f[...], fan(pg), 1, 1) + dot(r_f[...], rim_fan(pg), 1, 1)
    pack_one(ref, one_ref)


def grad_two(ref, s_c, r_c, hidden, two_ref):
    two_ref[...] = dot(fan(hidden), s_c[...], 1, 1) + dot(rim_fan(hidden), r_c[...], 1, 1)
    pack_two(ref, two_ref)


def send_kernel(odd_ref, far_ref, near_ref, m_ref, s_send, wf, wb, pre_ref, hg_ref,
                send_ref, far_pg_ref, pg_ref, kept_ref, r_keep, r_send, one_ref, two_ref):
    chans, n = pg_ref.shape
    rim = slice(0, RIM)
    end = slice(RIM, 2 * RIM)
    first = send_ref.shape[0] - RIM // 2

    def own(ref, low, high):
        mid = ref[:, RIM : RIM + n]
        return jnp.concatenate([mid[:, :RIM] + low, mid[:, RIM : n - RIM], mid[:, n - RIM :] + high], 1)

    def work(even, r_f, r_c):
        far = jnp.where(odd_ref[0] >= 2, far_ref[...], jnp.zeros_like(far_ref))
        near = near_ref[...]
        both = jnp.concatenate([far, near] if even else [near, far], 1)
        write_shifts(r_f, both[:chans, :])
        write_shifts(r_c, both[chans:, :])
        low_pre = dot(wf[:chans, :], r_f[:, rim], 1, 0)
        high_pre = dot(wf[2 * chans :, :], r_f[:, end], 1, 0)
        low_hg = dot(wb[:chans, :], r_c[:, rim], 1, 0)
        high_hg = dot(wb[2 * chans :, :], r_c[:, end], 1, 0)
        mask = m_ref[0:1, :].astype(F32)
        hidden, pg = slope(own(hg_ref, low_hg, high_hg), own(pre_ref, low_pre, high_pre), mask)
        hidden = hidden.astype(BF)
        pg_ref[...] = pg
        if even:
            kept_ref[...] = pg
            grad_two(send_ref, s_send, r_c, hidden, two_ref)
        else:
            kept_ref[...] = hidden
            grad_one(send_ref, s_send, r_f, pg, one_ref)
        near_plane, far_plane = (n - RIM, 0) if even else (0, n - RIM)
        for i in range(RIM // (2 * chans)):
            lanes = slice(near_plane + 2 * i * chans, near_plane + 2 * (i + 1) * chans)
            send_ref[first + i * chans : first + (i + 1) * chans, :] = pg[:, lanes]
        far_pg_ref[...] = pg[:, far_plane : far_plane + RIM]

    @pl.when(odd_ref[0] % 2 == 0)
    def _():
        work(True, r_keep, r_send)

    @pl.when(odd_ref[0] % 2 != 0)
    def _():
        work(False, r_send, r_keep)


def keep_kernel(odd_ref, s_keep, rims, kept_ref, keep_ref, one_ref, two_ref):
    @pl.when(odd_ref[0] % 2 == 0)
    def _():
        grad_one(keep_ref, s_keep, rims, kept_ref[...], one_ref)

    @pl.when(odd_ref[0] % 2 != 0)
    def _():
        grad_two(keep_ref, s_keep, rims, kept_ref[...], two_ref)


def pack_one(ref, one_ref):
    taps, chans = one_ref.shape[0], one_ref.shape[1] // 3
    fold = taps // 2
    ref[:taps, :] = one_ref[:, : 2 * chans].astype(ref.dtype)
    last = one_ref[:, 2 * chans :].astype(ref.dtype)
    ref[taps : taps + fold, :chans] = last[:fold]
    ref[taps : taps + fold, chans:] = last[fold:]


def pack_two(ref, two_ref):
    deep, chans = two_ref.shape[0], two_ref.shape[0] // 3
    fold = deep // 2
    for t in range(4):
        ref[t * deep : (t + 1) * deep, :] = two_ref[:, 2 * t * chans : 2 * (t + 1) * chans].astype(ref.dtype)
    last = two_ref[:, 8 * chans :].astype(ref.dtype)
    ref[4 * deep : 4 * deep + fold, :chans] = last[:fold]
    ref[4 * deep : 4 * deep + fold, chans:] = last[fold:]


def unpack_one(src, dst, dz):
    chans = dst.shape[1]
    taps = 9 * chans
    fold = taps // 2
    for j in range(9):
        first, k = j * chans, dz * 9 + j
        if dz < 2:
            dst[k] = src[first : first + chans, dz * chans : (dz + 1) * chans].astype(F32)
            continue
        for begin in range(first, first + chans, chans // 2):
            row, lane = taps + begin % fold, begin // fold * chans
            at = begin - first
            dst[k, at : at + chans // 2, :] = src[row : row + chans // 2, lane : lane + chans].astype(F32)


def unpack_two(src, dst, dz):
    chans = dst.shape[1]
    deep = 3 * chans
    fold = deep // 2
    first = (2 - dz) * chans
    for j in range(9):
        mirror, k = 8 - j, dz * 9 + j
        if mirror < 8:
            row, lane = mirror // 2 * deep + first, mirror % 2 * chans
            dst[k] = src[row : row + chans, lane : lane + chans].astype(F32)
            continue
        for begin in range(first, first + chans, chans // 2):
            row, lane = 4 * deep + begin % fold, begin // fold * chans
            at = begin - first
            dst[k, at : at + chans // 2, :] = src[row : row + chans // 2, lane : lane + chans].astype(F32)


def write_half(src, one_hbm, two_hbm, wide, sems, is_one):
    def write(unpack, out):
        copies = []
        for dz in range(3):
            unpack(src, wide, dz)
            third = pl.ds(dz * 9, 9)
            copies.append(pltpu.make_async_copy(wide.at[third], out.at[third], sems.at[dz]))
            copies[-1].start()
        for copy in copies:
            copy.wait()

    @pl.when(is_one)
    def _():
        write(unpack_one, one_hbm)

    @pl.when(jnp.logical_not(is_one))
    def _():
        write(unpack_two, two_hbm)


def mine_kernel(odd_ref, src, one_hbm, two_hbm, wide, sems):
    write_half(src, one_hbm, two_hbm, wide, sems, odd_ref[0] % 2 == 0)


def yours_kernel(odd_ref, src, _one, _two, one_hbm, two_hbm, wide, sems):
    write_half(src, one_hbm, two_hbm, wide, sems, odd_ref[0] % 2 != 0)


def last_kernel(odd_ref, near_ref, far_ref, m_ref, pg_ref, w1_hbm, _, out_ref, zero_ref, s_p, wb, w1, sems):
    chans, n = pg_ref.shape
    weights = pltpu.make_async_copy(w1_hbm, w1, sems.at[0])
    weights.start()
    zero_ref[...] = jnp.zeros_like(zero_ref)
    first = near_ref.shape[0] - RIM // 2
    near = jnp.concatenate(
        [near_ref[first + i * chans : first + (i + 1) * chans, :] for i in range(RIM // (2 * chans))], 1
    )
    left, right = sides(odd_ref, near, far_ref[...])
    write_shifts(s_p, jnp.concatenate([left, pg_ref[...], right], 1))
    weights.wait()
    backward_weights(w1, wb, chans)
    out = join_planes(dot(wb[...], s_p[...], 1, 0), chans) * m_ref[0:1, :].astype(F32)
    out_ref[...] = out.astype(BF)


def whole(shape):
    return pl.BlockSpec(shape, lambda i: (0,) * len(shape))


HBM = pl.BlockSpec(memory_space=pltpu.HBM)
ANY = pl.BlockSpec(memory_space=pl.ANY)
SCALAR = pl.BlockSpec(memory_space=pltpu.SMEM)


def call(kernel, args, outs, scratch=(), specs=None, flops=0, out_specs=None, aliases=None):
    specs = specs or {}
    args = [
        pltpu.with_memory_space_constraint(x, pltpu.HBM) if specs.get(i) is HBM else x
        for i, x in enumerate(args)
    ]
    return pl.pallas_call(
        kernel,
        grid=(1,),
        in_specs=[specs.get(i, whole(x.shape)) for i, x in enumerate(args)],
        out_specs=out_specs or [whole(o.shape) for o in outs],
        input_output_aliases=aliases or {},
        out_shape=outs,
        scratch_shapes=list(scratch),
        compiler_params=pltpu.CompilerParams(vmem_limit_bytes=40 * 1024 * 1024),
        cost_estimate=pl.CostEstimate(flops=flops, bytes_accessed=0, transcendentals=0) if flops else None,
    )(*args)


def all_sum(keep, send, axis, beside):
    count = lax.axis_size(axis)
    me = lax.axis_index(axis)
    is_odd = (me & 1) > 0
    bits = [1 << i for i in range(1, count.bit_length() - 1)]
    even_bits, odd_bits = bits, bits[-1:] + bits[:-1]

    def swap(x, step):
        bit = (even_bits[step], odd_bits[step])
        return lax.ppermute(x, axis, [(i, i ^ bit[i & 1]) for i in range(count)])

    def neighbour(x):
        return lax.ppermute(x, axis, [(i, i ^ 1) for i in range(count)])

    came = neighbour(send)
    cur = keep + came[: keep.shape[0]].astype(F32)
    upper = (me & jnp.where(is_odd, odd_bits[0], even_bits[0])) > 0
    n = cur.shape[0] // 2
    low, high = cur[:n], cur[n:]
    cur = jnp.where(upper, high, low) + swap(jnp.where(upper, low, high).astype(BF), 0).astype(F32)
    for step in range(1, len(bits)):
        sent = cur.astype(BF)
        other = swap(sent, step)
        if step == len(bits) - 1:
            zero = beside(came, sent)
        cur = sent.astype(F32) + other.astype(F32)
    cur = (cur + zero).astype(BF)
    other = swap(cur, 0)
    cur = jnp.concatenate([jnp.where(upper, other, cur), jnp.where(upper, cur, other)], 0)
    return cur, neighbour(cur)


def far_partners(parts, count):
    pairs = []
    for part in range(parts):
        base = part * count
        for i in range(1, count - 1, 2):
            pairs += [(base + i, base + i + 1), (base + i + 1, base + i)]
        other = part ^ 1
        if other < parts:
            pairs += [(base, other * count), (base + count - 1, other * count + count - 1)]
    return pairs


def on_device(features, weight_one, weight_two, rules, cotangent):
    rows, chans = features.shape
    koff = rules.shape[1]
    ft, ct, rt = features.T, cotangent.T, rules.T
    count = lax.axis_size("slab")
    me = lax.axis_index("slab")
    inner = (me > 0) & (me < count - 1)
    odd = (me % 2 + 2 * inner.astype(me.dtype)).astype(jnp.int32).reshape(1)

    def array(*shape, kind=BF):
        return jax.ShapeDtypeStruct(shape, kind)

    def dma(n):
        return pltpu.SemaphoreType.DMA((n,))

    halo = (2 * chans, RIM)
    taps = 9 * chans
    weights = pltpu.VMEM(weight_one.shape, BF)
    near, far, f, c, m = call(
        prep_kernel,
        (odd, ft, ct, rt),
        [array(*halo), array(*halo), array(chans, rows), array(chans, rows), array(16, rows)],
        [pltpu.VMEM((8, rows), jnp.int32), dma(3)],
        {0: SCALAR, 1: HBM, 2: HBM, 3: HBM},
    )
    far_pairs = far_partners(lax.axis_size("parts"), count)
    near_pairs = [(i, i ^ 1) for i in range(count)]
    near_in = lax.ppermute(near, "slab", near_pairs)
    far_in = lax.ppermute(far, ("parts", "slab"), far_pairs)
    s_keep, s_send, wf, wb, pre, hg = call(
        own_kernel,
        (odd, f, c, weight_one, weight_two),
        [array(taps, rows), array(taps, rows), array(3 * chans, taps), array(3 * chans, taps),
         array(chans, rows + 2 * RIM, kind=F32), array(chans, rows + 2 * RIM, kind=F32)],
        [weights, weights, pltpu.VMEM((taps, 3 * chans), BF), dma(2)],
        {0: SCALAR, 3: HBM, 4: HBM},
        flops=2 * 2 * rows * koff * chans * chans,
    )
    half = koff * chans // 2
    grad_scratch = [pltpu.VMEM((taps, 3 * chans), F32), pltpu.VMEM((3 * chans, taps), F32)]
    send, far_pg, pg, kept, rims = call(
        send_kernel,
        (odd, far_in, near_in, m, s_send, wf, wb, pre, hg),
        [array(half + RIM // 2, 2 * chans), array(chans, RIM), array(chans, rows), array(chans, rows),
         array(taps, 2 * RIM)],
        [pltpu.VMEM((taps, 2 * RIM), BF), *grad_scratch],
        {0: SCALAR},
        flops=2 * 2 * rows * koff * chans * chans,
    )
    (keep,) = call(
        keep_kernel,
        (odd, s_keep, rims, kept),
        [array(half, 2 * chans, kind=F32)],
        grad_scratch,
        {0: SCALAR},
        flops=2 * rows * koff * chans * chans,
    )
    far_pg = lax.ppermute(far_pg, ("parts", "slab"), far_pairs)
    done = []

    def beside(came, sent):
        fg, zero = call(
            last_kernel,
            (odd, came, far_pg, m, pg, weight_one, sent),
            [array(chans, rows), array(8, 2 * chans, kind=F32)],
            [pltpu.VMEM((taps, rows + 2 * RIM), BF), pltpu.VMEM((3 * chans, taps), BF), weights, dma(1)],
            {0: SCALAR, 5: HBM, 6: ANY},
            flops=2 * 2 * rows * koff * chans * chans,
        )
        done.append(fg)
        return zero[:1]

    mine, yours = all_sum(keep, send, "slab", beside)
    grads = [array(koff, chans, chans, kind=F32)] * 2
    scratch = [pltpu.VMEM((koff, chans, chans), F32), dma(3)]
    grads_out = call(
        mine_kernel, (odd, mine), grads, scratch, {0: SCALAR}, flops=2 * rows * koff * chans * chans,
        out_specs=[ANY, ANY],
    )
    first_grad, second_grad = call(
        yours_kernel, (odd, yours, *grads_out), grads, scratch, {0: SCALAR, 2: ANY, 3: ANY},
        out_specs=[ANY, ANY], aliases={2: 0, 3: 1},
    )
    return done[0].T, first_grad, second_grad


def solution(mesh):
    return jax.shard_map(
        on_device,
        mesh=mesh,
        in_specs=(
            P(("parts", "slab"), None),
            P(),
            P(),
            P(("parts", "slab"), None),
            P(("parts", "slab"), None),
        ),
        out_specs=(P(("parts", "slab"), None), P("parts", None, None), P("parts", None, None)),
        check_vma=False,
    )
```

```python
import functools

import jax
import jax.numpy as jnp
from jax import lax
from jax.experimental import pallas as pl
from jax.experimental.pallas import tpu as pltpu
from jax.sharding import PartitionSpec as P

SIDE = 16
RIM = SIDE * SIDE
BF = jnp.bfloat16
F32 = jnp.float32
OFFSETS = [dy * SIDE + dx for dy in (-1, 0, 1) for dx in (-1, 0, 1)]


def edge_masks(length):
    lane = lax.broadcasted_iota(jnp.int32, (1, length), 1)
    x, y = lane % SIDE, (lane // SIDE) % SIDE
    inside = {}
    for dy in (-1, 0, 1):
        for dx in (-1, 0, 1):
            ok = (x + dx >= 0) & (x + dx < SIDE) & (y + dy >= 0) & (y + dy < SIDE)
            inside[dy * SIDE + dx] = jnp.where(ok, 1.0, 0.0).astype(BF)
    return inside


def write_shifts(dst, values):
    length = values.shape[1]
    inside = edge_masks(length)
    chans = values.shape[0]
    for j, off in enumerate(OFFSETS):
        moved = values if off == 0 else pltpu.roll(values, (-off) % length, 1) * inside[off]
        dst[j * chans : (j + 1) * chans, :] = moved


def dot(a, b, ca, cb):
    return lax.dot_general(a, b, (((ca,), (cb,)), ((), ())), preferred_element_type=F32)


def join_planes(terms, chans):
    n = terms.shape[1]
    return (
        terms[:chans, : n - 2 * RIM]
        + terms[chans : 2 * chans, RIM : n - RIM]
        + terms[2 * chans :, 2 * RIM :]
    )


def backward_weights(w_ref, dst, chans):
    for dz in range(3):
        for j in range(9):
            dst[dz * chans : (dz + 1) * chans, j * chans : (j + 1) * chans] = w_ref[26 - (dz * 9 + j)]


def forward_weights(w_ref, dst, chans):
    for dz in range(3):
        for j in range(9):
            dst[j * chans : (j + 1) * chans, dz * chans : (dz + 1) * chans] = w_ref[dz * 9 + j]


def prep_kernel(odd_ref, f_hbm, c_hbm, r_hbm, near_ref, far_ref, f_ref, c_ref, m_ref, rules, sems):
    chans, n = f_ref.shape
    copies = [
        pltpu.make_async_copy(r_hbm.at[8:16, :], rules, sems.at[0]),
        pltpu.make_async_copy(f_hbm, f_ref, sems.at[1]),
        pltpu.make_async_copy(c_hbm, c_ref, sems.at[2]),
    ]
    for copy in copies:
        copy.start()
    copies[0].wait()
    mask = jnp.where(rules[5:6, :] >= 0, 1.0, 0.0).astype(BF)
    m_ref[...] = jnp.broadcast_to(mask, m_ref.shape)
    for copy in copies[1:]:
        copy.wait()
    f_ref[...] = f_ref[...] * mask
    c_ref[...] = c_ref[...] * mask
    odd = odd_ref[0] % 2

    def fill(ref, lanes):
        ref[:chans, :] = f_ref[:, lanes]
        ref[chans:, :] = c_ref[:, lanes]

    def fill_far(lanes, next_lanes):
        fill(far_ref.at[: 2 * chans, :], lanes)
        fill(far_ref.at[2 * chans : 4 * chans, :], next_lanes)
        far_ref[4 * chans :, :] = m_ref[:, lanes]

    first, last = slice(0, RIM), slice(n - RIM, n)

    @pl.when(odd == 0)
    def _():
        fill(near_ref, last)
        fill_far(first, slice(RIM, 2 * RIM))

    @pl.when(odd != 0)
    def _():
        fill(near_ref, first)
        fill_far(last, slice(n - 2 * RIM, n - RIM))


def own_kernel(odd_ref, f_ref, c_ref, w1_hbm, w2_hbm, s_keep, s_send, wf, wb, pre_ref, hg_ref, w1, w2, turned, sems):
    chans, n = f_ref.shape
    copies = [
        pltpu.make_async_copy(w1_hbm, w1, sems.at[0]),
        pltpu.make_async_copy(w2_hbm, w2, sems.at[1]),
    ]
    for copy in copies:
        copy.start()
    for copy in copies:
        copy.wait()

    def work(s_f, s_c):
        write_shifts(s_f, f_ref[...])
        write_shifts(s_c, c_ref[...])
        forward_weights(w1, turned, chans)
        wf[...] = turned[...].T
        spread_terms(pre_ref, dot(wf[...], s_f[...], 1, 0), chans)
        backward_weights(w2, wb, chans)
        spread_terms(hg_ref, dot(wb[...], s_c[...], 1, 0), chans)

    @pl.when(odd_ref[0] % 2 == 0)
    def _():
        work(s_keep, s_send)

    @pl.when(odd_ref[0] % 2 != 0)
    def _():
        work(s_send, s_keep)


def spread_terms(out_ref, terms, chans):
    n = terms.shape[1]
    low, mid, high = terms[:chans], terms[chans : 2 * chans], terms[2 * chans :]
    out_ref[:, :RIM] = high[:, :RIM]
    out_ref[:, RIM : 2 * RIM] = mid[:, :RIM] + high[:, RIM : 2 * RIM]
    out_ref[:, 2 * RIM : n] = mid[:, RIM : n - RIM] + high[:, 2 * RIM :] + low[:, : n - 2 * RIM]
    out_ref[:, n : n + RIM] = mid[:, n - RIM :] + low[:, n - 2 * RIM : n - RIM]
    out_ref[:, n + RIM :] = low[:, n - RIM :]


def sides(odd_ref, near, far):
    far = jnp.where(odd_ref[0] >= 2, far, jnp.zeros_like(far))
    even = odd_ref[0] % 2 == 0
    return jnp.where(even, far, near), jnp.where(even, near, far)


def slope(hg, pre, mask):
    sig = 1.0 / (1.0 + jnp.exp(-pre))
    return pre * sig * mask, (hg * mask * sig * (1.0 + pre * (1.0 - sig))).astype(BF)


def fan(v):
    blank = jnp.zeros((v.shape[0], RIM), BF)
    after = jnp.concatenate([v[:, RIM:], blank], 1)
    before = jnp.concatenate([blank, v[:, : v.shape[1] - RIM]], 1)
    return jnp.concatenate([after, v, before], 0)


def rim_fan(v):
    blank = jnp.zeros((v.shape[0], RIM), BF)
    first = jnp.concatenate([v[:, :RIM], blank], 1)
    last = jnp.concatenate([blank, v[:, v.shape[1] - RIM :]], 1)
    return jnp.concatenate([first, jnp.zeros_like(first), last], 0)


def grad_one(ref, s_f, r_f, pg, one_ref):
    one_ref[...] = dot(s_f[...], fan(pg), 1, 1) + dot(r_f[...], rim_fan(pg), 1, 1)
    pack_one(ref, one_ref)


def grad_two(ref, s_c, r_c, hidden, two_ref):
    two_ref[...] = dot(fan(hidden), s_c[...], 1, 1) + dot(rim_fan(hidden), r_c[...], 1, 1)
    pack_two(ref, two_ref)


def send_kernel(odd_ref, far_ref, near_ref, m_ref, s_send, wf, wb, pre_ref, hg_ref,
                send_ref, side_ref, pg_ref, kept_ref, r_keep, r_send, one_ref, two_ref):
    chans, n = pg_ref.shape
    rim = slice(0, RIM)
    end = slice(RIM, 2 * RIM)
    first = send_ref.shape[0] - RIM // 2

    def own(ref, low, high):
        mid = ref[:, RIM : RIM + n]
        return jnp.concatenate([mid[:, :RIM] + low, mid[:, RIM : n - RIM], mid[:, n - RIM :] + high], 1)

    def work(even, r_f, r_c):
        far = far_ref[: 2 * chans, :]
        far = jnp.where(odd_ref[0] >= 2, far, jnp.zeros_like(far))
        near = near_ref[...]
        both = jnp.concatenate([far, near] if even else [near, far], 1)
        write_shifts(r_f, both[:chans, :])
        write_shifts(r_c, both[chans:, :])
        low_pre = dot(wf[:chans, :], r_f[:, rim], 1, 0)
        high_pre = dot(wf[2 * chans :, :], r_f[:, end], 1, 0)
        low_hg = dot(wb[:chans, :], r_c[:, rim], 1, 0)
        high_hg = dot(wb[2 * chans :, :], r_c[:, end], 1, 0)
        mask = m_ref[0:1, :].astype(F32)
        hidden, pg = slope(own(hg_ref, low_hg, high_hg), own(pre_ref, low_pre, high_pre), mask)
        hidden = hidden.astype(BF)
        pg_ref[...] = pg
        if even:
            kept_ref[...] = pg
            grad_two(send_ref, s_send, r_c, hidden, two_ref)
        else:
            kept_ref[...] = hidden
            grad_one(send_ref, s_send, r_f, pg, one_ref)
        near_plane, beyond = (n - RIM, 0) if even else (0, n + RIM)
        side_ref[:chans, :] = pre_ref[:, beyond : beyond + RIM]
        side_ref[chans:, :] = hg_ref[:, beyond : beyond + RIM]
        for i in range(RIM // (2 * chans)):
            lanes = slice(near_plane + 2 * i * chans, near_plane + 2 * (i + 1) * chans)
            send_ref[first + i * chans : first + (i + 1) * chans, :] = pg[:, lanes]

    @pl.when(odd_ref[0] % 2 == 0)
    def _():
        work(True, r_keep, r_send)

    @pl.when(odd_ref[0] % 2 != 0)
    def _():
        work(False, r_send, r_keep)


def far_kernel(odd_ref, far_ref, side_ref, wf, wb, _, plane_ref, s_near, s_off):
    chans = plane_ref.shape[0]
    own, twice = slice(0, chans), slice(chans, 2 * chans)

    def work(even):
        edge = slice(0, chans) if even else slice(2 * chans, 3 * chans)

        def terms(w, rows):
            write_shifts(s_near, far_ref[rows, :])
            write_shifts(s_off, far_ref[rows.start + 2 * chans : rows.stop + 2 * chans, :])
            return side_ref[rows, :] + dot(w[edge, :], s_off[...], 1, 0) + dot(w[twice, :], s_near[...], 1, 0)

        mask = far_ref[4 * chans : 4 * chans + 1, :].astype(F32)
        pre = terms(wf, own)
        _, plane_ref[...] = slope(terms(wb, twice), pre, mask)

    @pl.when(odd_ref[0] % 2 == 0)
    def _():
        work(True)

    @pl.when(odd_ref[0] % 2 != 0)
    def _():
        work(False)


def keep_kernel(odd_ref, s_keep, rims, kept_ref, keep_ref, one_ref, two_ref):
    @pl.when(odd_ref[0] % 2 == 0)
    def _():
        grad_one(keep_ref, s_keep, rims, kept_ref[...], one_ref)

    @pl.when(odd_ref[0] % 2 != 0)
    def _():
        grad_two(keep_ref, s_keep, rims, kept_ref[...], two_ref)


def pack_one(ref, one_ref):
    taps, chans = one_ref.shape[0], one_ref.shape[1] // 3
    fold = taps // 2
    ref[:taps, :] = one_ref[:, : 2 * chans].astype(ref.dtype)
    last = one_ref[:, 2 * chans :].astype(ref.dtype)
    ref[taps : taps + fold, :chans] = last[:fold]
    ref[taps : taps + fold, chans:] = last[fold:]


def pack_two(ref, two_ref):
    deep, chans = two_ref.shape[0], two_ref.shape[0] // 3
    fold = deep // 2
    for t in range(4):
        ref[t * deep : (t + 1) * deep, :] = two_ref[:, 2 * t * chans : 2 * (t + 1) * chans].astype(ref.dtype)
    last = two_ref[:, 8 * chans :].astype(ref.dtype)
    ref[4 * deep : 4 * deep + fold, :chans] = last[:fold]
    ref[4 * deep : 4 * deep + fold, chans:] = last[fold:]


def unpack_one(src, dst, dz):
    chans = dst.shape[1]
    taps = 9 * chans
    fold = taps // 2
    for j in range(9):
        first, k = j * chans, dz * 9 + j
        if dz < 2:
            dst[k] = src[first : first + chans, dz * chans : (dz + 1) * chans].astype(F32)
            continue
        for begin in range(first, first + chans, chans // 2):
            row, lane = taps + begin % fold, begin // fold * chans
            at = begin - first
            dst[k, at : at + chans // 2, :] = src[row : row + chans // 2, lane : lane + chans].astype(F32)


def unpack_two(src, dst, dz):
    chans = dst.shape[1]
    deep = 3 * chans
    fold = deep // 2
    first = (2 - dz) * chans
    for j in range(9):
        mirror, k = 8 - j, dz * 9 + j
        if mirror < 8:
            row, lane = mirror // 2 * deep + first, mirror % 2 * chans
            dst[k] = src[row : row + chans, lane : lane + chans].astype(F32)
            continue
        for begin in range(first, first + chans, chans // 2):
            row, lane = 4 * deep + begin % fold, begin // fold * chans
            at = begin - first
            dst[k, at : at + chans // 2, :] = src[row : row + chans // 2, lane : lane + chans].astype(F32)


def write_half(src, one_hbm, two_hbm, wide, sems, is_one):
    def write(unpack, out):
        copies = []
        for dz in range(3):
            unpack(src, wide, dz)
            third = pl.ds(dz * 9, 9)
            copies.append(pltpu.make_async_copy(wide.at[third], out.at[third], sems.at[dz]))
            copies[-1].start()
        for copy in copies:
            copy.wait()

    @pl.when(is_one)
    def _():
        write(unpack_one, one_hbm)

    @pl.when(jnp.logical_not(is_one))
    def _():
        write(unpack_two, two_hbm)


def join(joined, parts):
    first = 0
    for part in parts:
        joined[first : first + part.shape[0], :] = part[...]
        first += part.shape[0]


def mine_kernel(odd_ref, part, rest, one_hbm, two_hbm, joined, wide, sems):
    join(joined, (part, rest))
    write_half(joined, one_hbm, two_hbm, wide, sems, odd_ref[0] % 2 == 0)


def yours_kernel(odd_ref, part, rest, _one, _two, one_hbm, two_hbm, joined, wide, sems):
    join(joined, (part, rest))
    write_half(joined, one_hbm, two_hbm, wide, sems, odd_ref[0] % 2 != 0)


def last_kernel(odd_ref, near_ref, far_ref, m_ref, pg_ref, w1_hbm, _, out_ref, zero_ref, s_p, wb, w1, sems):
    chans, n = pg_ref.shape
    weights = pltpu.make_async_copy(w1_hbm, w1, sems.at[0])
    weights.start()
    zero_ref[...] = jnp.zeros_like(zero_ref)
    first = near_ref.shape[0] - RIM // 2
    near = jnp.concatenate(
        [near_ref[first + i * chans : first + (i + 1) * chans, :] for i in range(RIM // (2 * chans))], 1
    )
    left, right = sides(odd_ref, near, far_ref[...])
    write_shifts(s_p, jnp.concatenate([left, pg_ref[...], right], 1))
    weights.wait()
    backward_weights(w1, wb, chans)
    out = join_planes(dot(wb[...], s_p[...], 1, 0), chans) * m_ref[0:1, :].astype(F32)
    out_ref[...] = out.astype(BF)


def whole(shape):
    return pl.BlockSpec(shape, lambda i: (0,) * len(shape))


HBM = pl.BlockSpec(memory_space=pltpu.HBM)
ANY = pl.BlockSpec(memory_space=pl.ANY)
SCALAR = pl.BlockSpec(memory_space=pltpu.SMEM)


def call(kernel, args, outs, scratch=(), specs=None, flops=0, out_specs=None, aliases=None):
    specs = specs or {}
    args = [
        pltpu.with_memory_space_constraint(x, pltpu.HBM) if specs.get(i) is HBM else x
        for i, x in enumerate(args)
    ]
    return pl.pallas_call(
        kernel,
        grid=(1,),
        in_specs=[specs.get(i, whole(x.shape)) for i, x in enumerate(args)],
        out_specs=out_specs or [whole(o.shape) for o in outs],
        input_output_aliases=aliases or {},
        out_shape=outs,
        scratch_shapes=list(scratch),
        compiler_params=pltpu.CompilerParams(vmem_limit_bytes=40 * 1024 * 1024),
        cost_estimate=pl.CostEstimate(flops=flops, bytes_accessed=0, transcendentals=0) if flops else None,
    )(*args)


def all_sum(keep, send, axis, beside):
    count = lax.axis_size(axis)
    bits = [1 << i for i in range(1, count.bit_length() - 1)]
    even_bits, odd_bits = bits, bits[-1:] + bits[:-1]

    def swap(x, step):
        bit = (even_bits[step], odd_bits[step])
        return lax.ppermute(x, axis, [(i, i ^ bit[i & 1]) for i in range(count)])

    def neighbour(x):
        return lax.ppermute(x, axis, [(i, i ^ 1) for i in range(count)])

    came = neighbour(send)
    rows = keep.shape[0]
    split = rows * 9 // 16 // 16 * 16
    whole_half = keep + came[:rows].astype(F32)
    parts = [whole_half[:split], whole_half[split:]]
    lasts = [None, None]
    for step in range(len(bits)):
        for i, part in enumerate(parts):
            sent = part.astype(BF)
            other = swap(sent, step)
            parts[i] = sent.astype(F32) + other.astype(F32)
            lasts[i] = sent
    zero = beside(came, lasts[0])
    parts = [(parts[0] + zero).astype(BF), parts[1].astype(BF)]
    return parts, [neighbour(part) for part in parts]


def far_partners(parts, count):
    pairs = []
    for part in range(parts):
        base = part * count
        for i in range(1, count - 1, 2):
            pairs += [(base + i, base + i + 1), (base + i + 1, base + i)]
        other = part ^ 1
        if other < parts:
            pairs += [(base, other * count), (base + count - 1, other * count + count - 1)]
    return pairs


def on_device(features, weight_one, weight_two, rules, cotangent):
    rows, chans = features.shape
    koff = rules.shape[1]
    ft, ct, rt = features.T, cotangent.T, rules.T
    count = lax.axis_size("slab")
    me = lax.axis_index("slab")
    inner = (me > 0) & (me < count - 1)
    odd = (me % 2 + 2 * inner.astype(me.dtype)).astype(jnp.int32).reshape(1)

    def array(*shape, kind=BF):
        return jax.ShapeDtypeStruct(shape, kind)

    def dma(n):
        return pltpu.SemaphoreType.DMA((n,))

    halo = (2 * chans, RIM)
    taps = 9 * chans
    weights = pltpu.VMEM(weight_one.shape, BF)
    near, far, f, c, m = call(
        prep_kernel,
        (odd, ft, ct, rt),
        [array(*halo), array(4 * chans + 16, RIM), array(chans, rows), array(chans, rows), array(16, rows)],
        [pltpu.VMEM((8, rows), jnp.int32), dma(3)],
        {0: SCALAR, 1: HBM, 2: HBM, 3: HBM},
    )
    far_pairs = far_partners(lax.axis_size("parts"), count)
    near_pairs = [(i, i ^ 1) for i in range(count)]
    near_in = lax.ppermute(near, "slab", near_pairs)
    far_in = lax.ppermute(far, ("parts", "slab"), far_pairs)
    s_keep, s_send, wf, wb, pre, hg = call(
        own_kernel,
        (odd, f, c, weight_one, weight_two),
        [array(taps, rows), array(taps, rows), array(3 * chans, taps), array(3 * chans, taps),
         array(chans, rows + 2 * RIM, kind=F32), array(chans, rows + 2 * RIM, kind=F32)],
        [weights, weights, pltpu.VMEM((taps, 3 * chans), BF), dma(2)],
        {0: SCALAR, 3: HBM, 4: HBM},
        flops=2 * 2 * rows * koff * chans * chans,
    )
    half = koff * chans // 2
    grad_scratch = [pltpu.VMEM((taps, 3 * chans), F32), pltpu.VMEM((3 * chans, taps), F32)]
    send, side, pg, kept, rims = call(
        send_kernel,
        (odd, far_in, near_in, m, s_send, wf, wb, pre, hg),
        [array(half + RIM // 2, 2 * chans), array(2 * chans, RIM, kind=F32), array(chans, rows), array(chans, rows),
         array(taps, 2 * RIM)],
        [pltpu.VMEM((taps, 2 * RIM), BF), *grad_scratch],
        {0: SCALAR},
        flops=2 * 2 * rows * koff * chans * chans,
    )
    (keep,) = call(
        keep_kernel,
        (odd, s_keep, rims, kept),
        [array(half, 2 * chans, kind=F32)],
        grad_scratch,
        {0: SCALAR},
        flops=2 * rows * koff * chans * chans,
    )
    done = []

    def beside(came, sent):
        (plane,) = call(
            far_kernel,
            (odd, far_in, side, wf, wb, sent),
            [array(chans, RIM)],
            [pltpu.VMEM((taps, RIM), BF), pltpu.VMEM((taps, RIM), BF)],
            {0: SCALAR, 5: ANY},
            flops=2 * RIM * koff * chans * chans,
        )
        fg, zero = call(
            last_kernel,
            (odd, came, plane, m, pg, weight_one, sent),
            [array(chans, rows), array(8, 2 * chans, kind=F32)],
            [pltpu.VMEM((taps, rows + 2 * RIM), BF), pltpu.VMEM((3 * chans, taps), BF), weights, dma(1)],
            {0: SCALAR, 5: HBM, 6: ANY},
            flops=2 * 2 * rows * koff * chans * chans,
        )
        done.append(fg)
        return zero[:1]

    mine, yours = all_sum(keep, send, "slab", beside)
    grads = [array(koff, chans, chans, kind=F32)] * 2
    scratch = [pltpu.VMEM((half, 2 * chans), BF), pltpu.VMEM((koff, chans, chans), F32), dma(3)]
    grads_out = call(
        mine_kernel, (odd, *mine), grads, scratch, {0: SCALAR}, flops=2 * rows * koff * chans * chans,
        out_specs=[ANY, ANY],
    )
    first_grad, second_grad = call(
        yours_kernel, (odd, *yours, *grads_out), grads, scratch, {0: SCALAR, 3: ANY, 4: ANY},
        out_specs=[ANY, ANY], aliases={3: 0, 4: 1},
    )
    return done[0].T, first_grad, second_grad


def solution(mesh):
    return jax.shard_map(
        on_device,
        mesh=mesh,
        in_specs=(
            P(("parts", "slab"), None),
            P(),
            P(),
            P(("parts", "slab"), None),
            P(("parts", "slab"), None),
        ),
        out_specs=(P(("parts", "slab"), None), P("parts", None, None), P("parts", None, None)),
        check_vma=False,
    )
```

```python
import functools

import jax
import jax.numpy as jnp
from jax import lax
from jax.experimental import pallas as pl
from jax.experimental.pallas import tpu as pltpu
from jax.sharding import PartitionSpec as P

SIDE = 16
RIM = SIDE * SIDE
BF = jnp.bfloat16
F32 = jnp.float32
OFFSETS = [dy * SIDE + dx for dy in (-1, 0, 1) for dx in (-1, 0, 1)]


def edge_masks(length):
    lane = lax.broadcasted_iota(jnp.int32, (1, length), 1)
    x, y = lane % SIDE, (lane // SIDE) % SIDE
    inside = {}
    for dy in (-1, 0, 1):
        for dx in (-1, 0, 1):
            ok = (x + dx >= 0) & (x + dx < SIDE) & (y + dy >= 0) & (y + dy < SIDE)
            inside[dy * SIDE + dx] = jnp.where(ok, 1.0, 0.0).astype(BF)
    return inside


def write_shifts(dst, values):
    length = values.shape[1]
    inside = edge_masks(length)
    chans = values.shape[0]
    for j, off in enumerate(OFFSETS):
        moved = values if off == 0 else pltpu.roll(values, (-off) % length, 1) * inside[off]
        dst[j * chans : (j + 1) * chans, :] = moved


def dot(a, b, ca, cb):
    return lax.dot_general(a, b, (((ca,), (cb,)), ((), ())), preferred_element_type=F32)


def join_planes(terms, chans):
    n = terms.shape[1]
    return (
        terms[:chans, : n - 2 * RIM]
        + terms[chans : 2 * chans, RIM : n - RIM]
        + terms[2 * chans :, 2 * RIM :]
    )


def backward_weights(w_ref, dst, chans):
    for dz in range(3):
        for j in range(9):
            dst[dz * chans : (dz + 1) * chans, j * chans : (j + 1) * chans] = w_ref[26 - (dz * 9 + j)]


def forward_weights(w_ref, dst, chans):
    for dz in range(3):
        for j in range(9):
            dst[j * chans : (j + 1) * chans, dz * chans : (dz + 1) * chans] = w_ref[dz * 9 + j]


def prep_kernel(odd_ref, f_hbm, c_hbm, r_hbm, near_ref, far_ref, f_ref, c_ref, m_ref, rules, sems):
    chans, n = f_ref.shape
    copies = [
        pltpu.make_async_copy(r_hbm.at[8:16, :], rules, sems.at[0]),
        pltpu.make_async_copy(f_hbm, f_ref, sems.at[1]),
        pltpu.make_async_copy(c_hbm, c_ref, sems.at[2]),
    ]
    for copy in copies:
        copy.start()
    copies[0].wait()
    mask = jnp.where(rules[5:6, :] >= 0, 1.0, 0.0).astype(BF)
    m_ref[...] = jnp.broadcast_to(mask, m_ref.shape)
    for copy in copies[1:]:
        copy.wait()
    f_ref[...] = f_ref[...] * mask
    c_ref[...] = c_ref[...] * mask
    odd = odd_ref[0] % 2

    def fill(ref, lanes):
        ref[:chans, :] = f_ref[:, lanes]
        ref[chans:, :] = c_ref[:, lanes]

    def fill_far(lanes, next_lanes):
        fill(far_ref.at[: 2 * chans, :], lanes)
        fill(far_ref.at[2 * chans : 4 * chans, :], next_lanes)
        far_ref[4 * chans :, :] = m_ref[:, lanes]

    first, last = slice(0, RIM), slice(n - RIM, n)

    @pl.when(odd == 0)
    def _():
        fill(near_ref, last)
        fill_far(first, slice(RIM, 2 * RIM))

    @pl.when(odd != 0)
    def _():
        fill(near_ref, first)
        fill_far(last, slice(n - 2 * RIM, n - RIM))


def own_kernel(odd_ref, f_ref, c_ref, w1_hbm, w2_hbm, s_keep, s_send, wf, wb, pre_ref, hg_ref, w1, w2, turned, sems):
    chans, n = f_ref.shape
    copies = [
        pltpu.make_async_copy(w1_hbm, w1, sems.at[0]),
        pltpu.make_async_copy(w2_hbm, w2, sems.at[1]),
    ]
    for copy in copies:
        copy.start()
    for copy in copies:
        copy.wait()

    def work(s_f, s_c):
        write_shifts(s_f, f_ref[...])
        write_shifts(s_c, c_ref[...])
        forward_weights(w1, turned, chans)
        wf[...] = turned[...].T
        spread_terms(pre_ref, dot(wf[...], s_f[...], 1, 0), chans)
        backward_weights(w2, wb, chans)
        spread_terms(hg_ref, dot(wb[...], s_c[...], 1, 0), chans)

    @pl.when(odd_ref[0] % 2 == 0)
    def _():
        work(s_keep, s_send)

    @pl.when(odd_ref[0] % 2 != 0)
    def _():
        work(s_send, s_keep)


def spread_terms(out_ref, terms, chans):
    n = terms.shape[1]
    low, mid, high = terms[:chans], terms[chans : 2 * chans], terms[2 * chans :]
    out_ref[:, :RIM] = high[:, :RIM]
    out_ref[:, RIM : 2 * RIM] = mid[:, :RIM] + high[:, RIM : 2 * RIM]
    out_ref[:, 2 * RIM : n] = mid[:, RIM : n - RIM] + high[:, 2 * RIM :] + low[:, : n - 2 * RIM]
    out_ref[:, n : n + RIM] = mid[:, n - RIM :] + low[:, n - 2 * RIM : n - RIM]
    out_ref[:, n + RIM :] = low[:, n - RIM :]


def sides(odd_ref, near, far):
    far = jnp.where(odd_ref[0] >= 2, far, jnp.zeros_like(far))
    even = odd_ref[0] % 2 == 0
    return jnp.where(even, far, near), jnp.where(even, near, far)


def slope(hg, pre, mask):
    sig = 1.0 / (1.0 + jnp.exp(-pre))
    return pre * sig * mask, (hg * mask * sig * (1.0 + pre * (1.0 - sig))).astype(BF)


def fan(v):
    blank = jnp.zeros((v.shape[0], RIM), BF)
    after = jnp.concatenate([v[:, RIM:], blank], 1)
    before = jnp.concatenate([blank, v[:, : v.shape[1] - RIM]], 1)
    return jnp.concatenate([after, v, before], 0)


def rim_fan(v):
    blank = jnp.zeros((v.shape[0], RIM), BF)
    first = jnp.concatenate([v[:, :RIM], blank], 1)
    last = jnp.concatenate([blank, v[:, v.shape[1] - RIM :]], 1)
    return jnp.concatenate([first, jnp.zeros_like(first), last], 0)


def grad_one(ref, s_f, r_f, pg, one_ref):
    one_ref[...] = dot(s_f[...], fan(pg), 1, 1) + dot(r_f[...], rim_fan(pg), 1, 1)
    pack_one(ref, one_ref)


def grad_two(ref, s_c, r_c, hidden, two_ref):
    two_ref[...] = dot(fan(hidden), s_c[...], 1, 1) + dot(rim_fan(hidden), r_c[...], 1, 1)
    pack_two(ref, two_ref)


def near_kernel(odd_ref, near_ref, m_ref, wf, wb, pre_ref, hg_ref, r_keep, r_send, hid_ref, pg_ref):
    chans, n = pg_ref.shape

    def work(even, r_f, r_c):
        write_shifts(r_f, near_ref[:chans, :])
        write_shifts(r_c, near_ref[chans:, :])
        edge = slice(2 * chans, 3 * chans) if even else slice(0, chans)
        first = RIM if even else 0

        def own(ref, more):
            part = ref[:, RIM + first : first + n]
            if even:
                return jnp.concatenate([part[:, : n - 2 * RIM], part[:, n - 2 * RIM :] + more], 1)
            return jnp.concatenate([part[:, :RIM] + more, part[:, RIM:]], 1)

        pre = own(pre_ref, dot(wf[edge, :], r_f[...], 1, 0))
        hg = own(hg_ref, dot(wb[edge, :], r_c[...], 1, 0))
        lanes = slice(first, first + n - RIM)
        hidden, pg = slope(hg, pre, m_ref[0:1, lanes].astype(F32))
        far = slice(0, RIM) if even else slice(n - RIM, n)
        hid_ref[:, lanes] = hidden.astype(BF)
        pg_ref[:, lanes] = pg
        hid_ref[:, far] = jnp.zeros((chans, RIM), BF)
        pg_ref[:, far] = jnp.zeros((chans, RIM), BF)

    @pl.when(odd_ref[0] % 2 == 0)
    def _():
        work(True, r_keep, r_send)

    @pl.when(odd_ref[0] % 2 != 0)
    def _():
        work(False, r_send, r_keep)


def send_kernel(odd_ref, far_ref, m_ref, s_send, wf, wb, pre_ref, hg_ref, near_keep, near_send, hid_part, pg_part,
                send_ref, side_ref, pg_ref, kept_ref, r_keep, r_send, one_ref, two_ref):
    chans, n = pg_ref.shape
    first = send_ref.shape[0] - RIM // 2

    def work(even, r_f, r_c):
        rim, end = slice(0, RIM), slice(RIM, 2 * RIM)
        far_lanes, near_lanes = (rim, end) if even else (end, rim)
        far = far_ref[: 2 * chans, :]
        far = jnp.where(odd_ref[0] >= 2, far, jnp.zeros_like(far))
        write_shifts(r_f.at[:, far_lanes], far[:chans, :])
        write_shifts(r_c.at[:, far_lanes], far[chans:, :])
        r_keep[:, near_lanes] = near_keep[...]
        r_send[:, near_lanes] = near_send[...]
        edge = slice(0, chans) if even else slice(2 * chans, 3 * chans)
        own = slice(RIM, 2 * RIM) if even else slice(n, n + RIM)
        pre = pre_ref[:, own] + dot(wf[edge, :], r_f[:, far_lanes], 1, 0)
        hg = hg_ref[:, own] + dot(wb[edge, :], r_c[:, far_lanes], 1, 0)
        hidden, pg = slope(hg, pre, m_ref[0:1, own.start - RIM : own.stop - RIM].astype(F32))
        hidden = hidden.astype(BF)
        if even:
            hidden = jnp.concatenate([hidden, hid_part[:, RIM:]], 1)
            pg = jnp.concatenate([pg, pg_part[:, RIM:]], 1)
        else:
            hidden = jnp.concatenate([hid_part[:, : n - RIM], hidden], 1)
            pg = jnp.concatenate([pg_part[:, : n - RIM], pg], 1)
        pg_ref[...] = pg
        if even:
            kept_ref[...] = pg
            grad_two(send_ref, s_send, r_c, hidden, two_ref)
        else:
            kept_ref[...] = hidden
            grad_one(send_ref, s_send, r_f, pg, one_ref)
        near_plane, beyond = (n - RIM, 0) if even else (0, n + RIM)
        side_ref[:chans, :] = pre_ref[:, beyond : beyond + RIM]
        side_ref[chans:, :] = hg_ref[:, beyond : beyond + RIM]
        for i in range(RIM // (2 * chans)):
            lanes = slice(near_plane + 2 * i * chans, near_plane + 2 * (i + 1) * chans)
            send_ref[first + i * chans : first + (i + 1) * chans, :] = pg[:, lanes]

    @pl.when(odd_ref[0] % 2 == 0)
    def _():
        work(True, r_keep, r_send)

    @pl.when(odd_ref[0] % 2 != 0)
    def _():
        work(False, r_send, r_keep)


def far_plane(even, far_ref, side_ref, wf, wb, plane_ref, s_near, s_off):
    chans = plane_ref.shape[0]
    own, twice = slice(0, chans), slice(chans, 2 * chans)
    edge = slice(0, chans) if even else slice(2 * chans, 3 * chans)

    def terms(w, rows):
        write_shifts(s_near, far_ref[rows, :])
        write_shifts(s_off, far_ref[rows.start + 2 * chans : rows.stop + 2 * chans, :])
        return side_ref[rows, :] + dot(w[edge, :], s_off[...], 1, 0) + dot(w[twice, :], s_near[...], 1, 0)

    mask = far_ref[4 * chans : 4 * chans + 1, :].astype(F32)
    pre = terms(wf, own)
    _, plane_ref[...] = slope(terms(wb, twice), pre, mask)


def keep_kernel(odd_ref, s_keep, rims, kept_ref, far_ref, side_ref, wf, wb, keep_ref, plane_ref,
                one_ref, two_ref, s_near, s_off):
    @pl.when(odd_ref[0] % 2 == 0)
    def _():
        grad_one(keep_ref, s_keep, rims, kept_ref[...], one_ref)
        far_plane(True, far_ref, side_ref, wf, wb, plane_ref, s_near, s_off)

    @pl.when(odd_ref[0] % 2 != 0)
    def _():
        grad_two(keep_ref, s_keep, rims, kept_ref[...], two_ref)
        far_plane(False, far_ref, side_ref, wf, wb, plane_ref, s_near, s_off)


def pack_one(ref, one_ref):
    taps, chans = one_ref.shape[0], one_ref.shape[1] // 3
    fold = taps // 2
    ref[:taps, :] = one_ref[:, : 2 * chans].astype(ref.dtype)
    last = one_ref[:, 2 * chans :].astype(ref.dtype)
    ref[taps : taps + fold, :chans] = last[:fold]
    ref[taps : taps + fold, chans:] = last[fold:]


def pack_two(ref, two_ref):
    deep, chans = two_ref.shape[0], two_ref.shape[0] // 3
    fold = deep // 2
    for t in range(4):
        ref[t * deep : (t + 1) * deep, :] = two_ref[:, 2 * t * chans : 2 * (t + 1) * chans].astype(ref.dtype)
    last = two_ref[:, 8 * chans :].astype(ref.dtype)
    ref[4 * deep : 4 * deep + fold, :chans] = last[:fold]
    ref[4 * deep : 4 * deep + fold, chans:] = last[fold:]


def unpack_one(src, dst, dz):
    chans = dst.shape[1]
    taps = 9 * chans
    fold = taps // 2
    for j in range(9):
        first, k = j * chans, dz * 9 + j
        if dz < 2:
            dst[k] = src[first : first + chans, dz * chans : (dz + 1) * chans].astype(F32)
            continue
        for begin in range(first, first + chans, chans // 2):
            row, lane = taps + begin % fold, begin // fold * chans
            at = begin - first
            dst[k, at : at + chans // 2, :] = src[row : row + chans // 2, lane : lane + chans].astype(F32)


def unpack_two(src, dst, dz):
    chans = dst.shape[1]
    deep = 3 * chans
    fold = deep // 2
    first = (2 - dz) * chans
    for j in range(9):
        mirror, k = 8 - j, dz * 9 + j
        if mirror < 8:
            row, lane = mirror // 2 * deep + first, mirror % 2 * chans
            dst[k] = src[row : row + chans, lane : lane + chans].astype(F32)
            continue
        for begin in range(first, first + chans, chans // 2):
            row, lane = 4 * deep + begin % fold, begin // fold * chans
            at = begin - first
            dst[k, at : at + chans // 2, :] = src[row : row + chans // 2, lane : lane + chans].astype(F32)


def write_half(src, one_hbm, two_hbm, wide, sems, is_one):
    def write(unpack, out):
        copies = []
        for dz in range(3):
            unpack(src, wide, dz)
            third = pl.ds(dz * 9, 9)
            copies.append(pltpu.make_async_copy(wide.at[third], out.at[third], sems.at[dz]))
            copies[-1].start()
        for copy in copies:
            copy.wait()

    @pl.when(is_one)
    def _():
        write(unpack_one, one_hbm)

    @pl.when(jnp.logical_not(is_one))
    def _():
        write(unpack_two, two_hbm)


def join(joined, parts):
    first = 0
    for part in parts:
        joined[first : first + part.shape[0], :] = part[...]
        first += part.shape[0]


def mine_kernel(odd_ref, part, rest, one_hbm, two_hbm, joined, wide, sems):
    join(joined, (part, rest))
    write_half(joined, one_hbm, two_hbm, wide, sems, odd_ref[0] % 2 == 0)


def yours_kernel(odd_ref, part, rest, _one, _two, one_hbm, two_hbm, joined, wide, sems):
    join(joined, (part, rest))
    write_half(joined, one_hbm, two_hbm, wide, sems, odd_ref[0] % 2 != 0)


def last_kernel(odd_ref, near_ref, far_ref, m_ref, pg_ref, w1_hbm, _, out_ref, zero_ref, s_p, wb, w1, sems):
    chans, n = pg_ref.shape
    weights = pltpu.make_async_copy(w1_hbm, w1, sems.at[0])
    weights.start()
    zero_ref[...] = jnp.zeros_like(zero_ref)
    first = near_ref.shape[0] - RIM // 2
    near = jnp.concatenate(
        [near_ref[first + i * chans : first + (i + 1) * chans, :] for i in range(RIM // (2 * chans))], 1
    )
    left, right = sides(odd_ref, near, far_ref[...])
    write_shifts(s_p, jnp.concatenate([left, pg_ref[...], right], 1))
    weights.wait()
    backward_weights(w1, wb, chans)
    out = join_planes(dot(wb[...], s_p[...], 1, 0), chans) * m_ref[0:1, :].astype(F32)
    out_ref[...] = out.astype(BF)


def zeros_after(_, zero_ref):
    zero_ref[...] = jnp.zeros_like(zero_ref)


def whole(shape):
    return pl.BlockSpec(shape, lambda i: (0,) * len(shape))


HBM = pl.BlockSpec(memory_space=pltpu.HBM)
ANY = pl.BlockSpec(memory_space=pl.ANY)
SCALAR = pl.BlockSpec(memory_space=pltpu.SMEM)


def call(kernel, args, outs, scratch=(), specs=None, flops=0, out_specs=None, aliases=None):
    specs = specs or {}
    args = [
        pltpu.with_memory_space_constraint(x, pltpu.HBM) if specs.get(i) is HBM else x
        for i, x in enumerate(args)
    ]
    return pl.pallas_call(
        kernel,
        grid=(1,),
        in_specs=[specs.get(i, whole(x.shape)) for i, x in enumerate(args)],
        out_specs=out_specs or [whole(o.shape) for o in outs],
        input_output_aliases=aliases or {},
        out_shape=outs,
        scratch_shapes=list(scratch),
        compiler_params=pltpu.CompilerParams(vmem_limit_bytes=40 * 1024 * 1024),
        cost_estimate=pl.CostEstimate(flops=flops, bytes_accessed=0, transcendentals=0) if flops else None,
    )(*args)


def all_sum(keep, send, axis, beside):
    count = lax.axis_size(axis)
    bits = [1 << i for i in range(1, count.bit_length() - 1)]
    even_bits, odd_bits = bits, bits[-1:] + bits[:-1]

    def swap(x, step):
        bit = (even_bits[step], odd_bits[step])
        return lax.ppermute(x, axis, [(i, i ^ bit[i & 1]) for i in range(count)])

    def neighbour(x):
        return lax.ppermute(x, axis, [(i, i ^ 1) for i in range(count)])

    came = neighbour(send)
    rows = keep.shape[0]
    split = rows * 9 // 16 // 16 * 16
    whole_half = keep + came[:rows].astype(F32)
    parts = [whole_half[:split], whole_half[split:]]
    for step in range(len(bits)):
        for i, part in enumerate(parts):
            sent = part.astype(BF)
            other = swap(sent, step)
            if step == len(bits) - 1 and i == 0:
                zero = beside(came, sent)
            parts[i] = sent.astype(F32) + other.astype(F32)
    second = parts[1].astype(BF)
    near_second = neighbour(second)
    (later,) = call(zeros_after, (near_second,), [jax.ShapeDtypeStruct((8, keep.shape[1]), F32)], specs={0: ANY})
    first = (parts[0] + zero + later[:1]).astype(BF)
    return [first, second], [neighbour(first), near_second]


def far_partners(parts, count):
    pairs = []
    for part in range(parts):
        base = part * count
        for i in range(1, count - 1, 2):
            pairs += [(base + i, base + i + 1), (base + i + 1, base + i)]
        other = part ^ 1
        if other < parts:
            pairs += [(base, other * count), (base + count - 1, other * count + count - 1)]
    return pairs


def on_device(features, weight_one, weight_two, rules, cotangent):
    rows, chans = features.shape
    koff = rules.shape[1]
    ft, ct, rt = features.T, cotangent.T, rules.T
    count = lax.axis_size("slab")
    me = lax.axis_index("slab")
    inner = (me > 0) & (me < count - 1)
    odd = (me % 2 + 2 * inner.astype(me.dtype)).astype(jnp.int32).reshape(1)

    def array(*shape, kind=BF):
        return jax.ShapeDtypeStruct(shape, kind)

    def dma(n):
        return pltpu.SemaphoreType.DMA((n,))

    halo = (2 * chans, RIM)
    taps = 9 * chans
    weights = pltpu.VMEM(weight_one.shape, BF)
    near, far, f, c, m = call(
        prep_kernel,
        (odd, ft, ct, rt),
        [array(*halo), array(4 * chans + 16, RIM), array(chans, rows), array(chans, rows), array(16, rows)],
        [pltpu.VMEM((8, rows), jnp.int32), dma(3)],
        {0: SCALAR, 1: HBM, 2: HBM, 3: HBM},
    )
    far_pairs = far_partners(lax.axis_size("parts"), count)
    near_pairs = [(i, i ^ 1) for i in range(count)]
    near_in = lax.ppermute(near, "slab", near_pairs)
    far_in = lax.ppermute(far, ("parts", "slab"), far_pairs)
    s_keep, s_send, wf, wb, pre, hg = call(
        own_kernel,
        (odd, f, c, weight_one, weight_two),
        [array(taps, rows), array(taps, rows), array(3 * chans, taps), array(3 * chans, taps),
         array(chans, rows + 2 * RIM, kind=F32), array(chans, rows + 2 * RIM, kind=F32)],
        [weights, weights, pltpu.VMEM((taps, 3 * chans), BF), dma(2)],
        {0: SCALAR, 3: HBM, 4: HBM},
        flops=2 * 2 * rows * koff * chans * chans,
    )
    half = koff * chans // 2
    grad_scratch = [pltpu.VMEM((taps, 3 * chans), F32), pltpu.VMEM((3 * chans, taps), F32)]
    near_keep, near_send, hid, pg = call(
        near_kernel,
        (odd, near_in, m, wf, wb, pre, hg),
        [array(taps, RIM), array(taps, RIM), array(chans, rows), array(chans, rows)],
        specs={0: SCALAR},
        flops=2 * RIM * koff * chans * chans,
    )
    send, side, pg, kept, rims = call(
        send_kernel,
        (odd, far_in, m, s_send, wf, wb, pre, hg, near_keep, near_send, hid, pg),
        [array(half + RIM // 2, 2 * chans), array(2 * chans, RIM, kind=F32), array(chans, rows), array(chans, rows),
         array(taps, 2 * RIM)],
        [pltpu.VMEM((taps, 2 * RIM), BF), *grad_scratch],
        {0: SCALAR},
        flops=2 * 2 * rows * koff * chans * chans,
    )
    keep, plane = call(
        keep_kernel,
        (odd, s_keep, rims, kept, far_in, side, wf, wb),
        [array(half, 2 * chans, kind=F32), array(chans, RIM)],
        [*grad_scratch, pltpu.VMEM((taps, RIM), BF), pltpu.VMEM((taps, RIM), BF)],
        {0: SCALAR},
        flops=2 * rows * koff * chans * chans,
    )
    done = []

    def beside(came, sent):
        fg, zero = call(
            last_kernel,
            (odd, came, plane, m, pg, weight_one, sent),
            [array(chans, rows), array(8, 2 * chans, kind=F32)],
            [pltpu.VMEM((taps, rows + 2 * RIM), BF), pltpu.VMEM((3 * chans, taps), BF), weights, dma(1)],
            {0: SCALAR, 5: HBM, 6: ANY},
            flops=2 * 2 * rows * koff * chans * chans,
        )
        done.append(fg)
        return zero[:1]

    mine, yours = all_sum(keep, send, "slab", beside)
    grads = [array(koff, chans, chans, kind=F32)] * 2
    scratch = [pltpu.VMEM((half, 2 * chans), BF), pltpu.VMEM((koff, chans, chans), F32), dma(3)]
    grads_out = call(
        mine_kernel, (odd, *mine), grads, scratch, {0: SCALAR}, flops=2 * rows * koff * chans * chans,
        out_specs=[ANY, ANY],
    )
    first_grad, second_grad = call(
        yours_kernel, (odd, *yours, *grads_out), grads, scratch, {0: SCALAR, 3: ANY, 4: ANY},
        out_specs=[ANY, ANY], aliases={3: 0, 4: 1},
    )
    return done[0].T, first_grad, second_grad


def solution(mesh):
    return jax.shard_map(
        on_device,
        mesh=mesh,
        in_specs=(
            P(("parts", "slab"), None),
            P(),
            P(),
            P(("parts", "slab"), None),
            P(("parts", "slab"), None),
        ),
        out_specs=(P(("parts", "slab"), None), P("parts", None, None), P("parts", None, None)),
        check_vma=False,
    )
```

```python
import functools

import jax
import jax.numpy as jnp
from jax import lax
from jax.experimental import pallas as pl
from jax.experimental.pallas import tpu as pltpu
from jax.sharding import PartitionSpec as P

SIDE = 16
RIM = SIDE * SIDE
BF = jnp.bfloat16
F32 = jnp.float32
OFFSETS = [dy * SIDE + dx for dy in (-1, 0, 1) for dx in (-1, 0, 1)]


def edge_masks(length):
    lane = lax.broadcasted_iota(jnp.int32, (1, length), 1)
    x, y = lane % SIDE, (lane // SIDE) % SIDE
    inside = {}
    for dy in (-1, 0, 1):
        for dx in (-1, 0, 1):
            ok = (x + dx >= 0) & (x + dx < SIDE) & (y + dy >= 0) & (y + dy < SIDE)
            inside[dy * SIDE + dx] = jnp.where(ok, 1.0, 0.0).astype(BF)
    return inside


def write_shifts(dst, values):
    length = values.shape[1]
    inside = edge_masks(length)
    chans = values.shape[0]
    for j, off in enumerate(OFFSETS):
        moved = values if off == 0 else pltpu.roll(values, (-off) % length, 1) * inside[off]
        dst[j * chans : (j + 1) * chans, :] = moved


def dot(a, b, ca, cb):
    return lax.dot_general(a, b, (((ca,), (cb,)), ((), ())), preferred_element_type=F32)


def join_planes(terms, chans):
    n = terms.shape[1]
    return (
        terms[:chans, : n - 2 * RIM]
        + terms[chans : 2 * chans, RIM : n - RIM]
        + terms[2 * chans :, 2 * RIM :]
    )


def backward_weights(w_ref, dst, chans):
    for dz in range(3):
        for j in range(9):
            dst[dz * chans : (dz + 1) * chans, j * chans : (j + 1) * chans] = w_ref[26 - (dz * 9 + j)]


def forward_weights(w_ref, dst, chans):
    for dz in range(3):
        for j in range(9):
            dst[j * chans : (j + 1) * chans, dz * chans : (dz + 1) * chans] = w_ref[dz * 9 + j]


def prep_kernel(odd_ref, f_hbm, c_hbm, r_hbm, near_ref, far_ref, f_ref, c_ref, m_ref, rules, sems):
    chans, n = f_ref.shape
    copies = [
        pltpu.make_async_copy(r_hbm.at[8:16, :], rules, sems.at[0]),
        pltpu.make_async_copy(f_hbm, f_ref, sems.at[1]),
        pltpu.make_async_copy(c_hbm, c_ref, sems.at[2]),
    ]
    for copy in copies:
        copy.start()
    copies[0].wait()
    mask = jnp.where(rules[5:6, :] >= 0, 1.0, 0.0).astype(BF)
    m_ref[...] = jnp.broadcast_to(mask, m_ref.shape)
    for copy in copies[1:]:
        copy.wait()
    f_ref[...] = f_ref[...] * mask
    c_ref[...] = c_ref[...] * mask
    odd = odd_ref[0] % 2

    def fill(ref, lanes):
        ref[:chans, :] = f_ref[:, lanes]
        ref[chans:, :] = c_ref[:, lanes]

    def fill_far(lanes, next_lanes):
        fill(far_ref.at[: 2 * chans, :], lanes)
        fill(far_ref.at[2 * chans : 4 * chans, :], next_lanes)
        far_ref[4 * chans :, :] = m_ref[:, lanes]

    first, last = slice(0, RIM), slice(n - RIM, n)

    @pl.when(odd == 0)
    def _():
        fill(near_ref, last)
        fill_far(first, slice(RIM, 2 * RIM))

    @pl.when(odd != 0)
    def _():
        fill(near_ref, first)
        fill_far(last, slice(n - 2 * RIM, n - RIM))


def own_kernel(odd_ref, f_ref, c_ref, w1_hbm, w2_hbm, s_keep, s_send, wf, wb, pre_ref, hg_ref, w1, w2, turned, sems):
    chans, n = f_ref.shape
    copies = [
        pltpu.make_async_copy(w1_hbm, w1, sems.at[0]),
        pltpu.make_async_copy(w2_hbm, w2, sems.at[1]),
    ]
    for copy in copies:
        copy.start()
    for copy in copies:
        copy.wait()

    def work(s_f, s_c):
        write_shifts(s_f, f_ref[...])
        write_shifts(s_c, c_ref[...])
        forward_weights(w1, turned, chans)
        wf[...] = turned[...].T
        spread_terms(pre_ref, dot(wf[...], s_f[...], 1, 0), chans)
        backward_weights(w2, wb, chans)
        spread_terms(hg_ref, dot(wb[...], s_c[...], 1, 0), chans)

    @pl.when(odd_ref[0] % 2 == 0)
    def _():
        work(s_keep, s_send)

    @pl.when(odd_ref[0] % 2 != 0)
    def _():
        work(s_send, s_keep)


def spread_terms(out_ref, terms, chans):
    n = terms.shape[1]
    low, mid, high = terms[:chans], terms[chans : 2 * chans], terms[2 * chans :]
    out_ref[:, :RIM] = high[:, :RIM]
    out_ref[:, RIM : 2 * RIM] = mid[:, :RIM] + high[:, RIM : 2 * RIM]
    out_ref[:, 2 * RIM : n] = mid[:, RIM : n - RIM] + high[:, 2 * RIM :] + low[:, : n - 2 * RIM]
    out_ref[:, n : n + RIM] = mid[:, n - RIM :] + low[:, n - 2 * RIM : n - RIM]
    out_ref[:, n + RIM :] = low[:, n - RIM :]


def sides(odd_ref, near, far):
    far = jnp.where(odd_ref[0] >= 2, far, jnp.zeros_like(far))
    even = odd_ref[0] % 2 == 0
    return jnp.where(even, far, near), jnp.where(even, near, far)


def slope(hg, pre, mask):
    sig = 1.0 / (1.0 + jnp.exp(-pre))
    return pre * sig * mask, (hg * mask * sig * (1.0 + pre * (1.0 - sig))).astype(BF)


def fan(v):
    blank = jnp.zeros((v.shape[0], RIM), BF)
    after = jnp.concatenate([v[:, RIM:], blank], 1)
    before = jnp.concatenate([blank, v[:, : v.shape[1] - RIM]], 1)
    return jnp.concatenate([after, v, before], 0)


def rim_fan(v):
    blank = jnp.zeros((v.shape[0], RIM), BF)
    first = jnp.concatenate([v[:, :RIM], blank], 1)
    last = jnp.concatenate([blank, v[:, v.shape[1] - RIM :]], 1)
    return jnp.concatenate([first, jnp.zeros_like(first), last], 0)


def grad_one(ref, s_f, r_f, pg, one_ref):
    one_ref[...] = dot(s_f[...], fan(pg), 1, 1) + dot(r_f[...], rim_fan(pg), 1, 1)
    pack_one(ref, one_ref)


def grad_two(ref, s_c, r_c, hidden, two_ref):
    two_ref[...] = dot(fan(hidden), s_c[...], 1, 1) + dot(rim_fan(hidden), r_c[...], 1, 1)
    pack_two(ref, two_ref)


def near_kernel(odd_ref, near_ref, m_ref, wf, wb, pre_ref, hg_ref, s_send, r_keep, r_send, hid_ref, pg_ref, one_ref, two_ref):
    chans, n = pg_ref.shape

    def work(even, r_f, r_c):
        write_shifts(r_f, near_ref[:chans, :])
        write_shifts(r_c, near_ref[chans:, :])
        edge = slice(2 * chans, 3 * chans) if even else slice(0, chans)
        first = RIM if even else 0

        def own(ref, more):
            part = ref[:, RIM + first : first + n]
            if even:
                return jnp.concatenate([part[:, : n - 2 * RIM], part[:, n - 2 * RIM :] + more], 1)
            return jnp.concatenate([part[:, :RIM] + more, part[:, RIM:]], 1)

        pre = own(pre_ref, dot(wf[edge, :], r_f[...], 1, 0))
        hg = own(hg_ref, dot(wb[edge, :], r_c[...], 1, 0))
        lanes = slice(first, first + n - RIM)
        hidden, pg = slope(hg, pre, m_ref[0:1, lanes].astype(F32))
        far = slice(0, RIM) if even else slice(n - RIM, n)
        hid_ref[:, lanes] = hidden.astype(BF)
        pg_ref[:, lanes] = pg
        hid_ref[:, far] = jnp.zeros((chans, RIM), BF)
        pg_ref[:, far] = jnp.zeros((chans, RIM), BF)
        if even:
            hidden = hid_ref[...]
            two_ref[...] = dot(fan(hidden), s_send[...], 1, 1)
            two_ref[2 * chans :, :] += dot(hidden[:, n - RIM :], r_c[...], 1, 1)
        else:
            pg = pg_ref[...]
            one_ref[...] = dot(s_send[...], fan(pg), 1, 1)
            one_ref[:, :chans] += dot(r_f[...], pg[:, :RIM], 1, 1)

    @pl.when(odd_ref[0] % 2 == 0)
    def _():
        work(True, r_keep, r_send)

    @pl.when(odd_ref[0] % 2 != 0)
    def _():
        work(False, r_send, r_keep)


def send_kernel(odd_ref, far_ref, m_ref, s_send, wf, wb, pre_ref, hg_ref, near_keep, near_send, hid_part, pg_part,
                one_part, two_part, send_ref, side_ref, pg_ref, kept_ref, r_keep, r_send, one_ref, two_ref):
    chans, n = pg_ref.shape
    first = send_ref.shape[0] - RIM // 2

    def work(even, r_f, r_c):
        rim, end = slice(0, RIM), slice(RIM, 2 * RIM)
        far_lanes, near_lanes = (rim, end) if even else (end, rim)
        far = far_ref[: 2 * chans, :]
        far = jnp.where(odd_ref[0] >= 2, far, jnp.zeros_like(far))
        write_shifts(r_f.at[:, far_lanes], far[:chans, :])
        write_shifts(r_c.at[:, far_lanes], far[chans:, :])
        r_keep[:, near_lanes] = near_keep[...]
        r_send[:, near_lanes] = near_send[...]
        edge = slice(0, chans) if even else slice(2 * chans, 3 * chans)
        own = slice(RIM, 2 * RIM) if even else slice(n, n + RIM)
        pre = pre_ref[:, own] + dot(wf[edge, :], r_f[:, far_lanes], 1, 0)
        hg = hg_ref[:, own] + dot(wb[edge, :], r_c[:, far_lanes], 1, 0)
        hidden, pg = slope(hg, pre, m_ref[0:1, own.start - RIM : own.stop - RIM].astype(F32))
        far_hidden, far_pg = hidden.astype(BF), pg
        hidden = far_hidden
        if even:
            hidden = jnp.concatenate([hidden, hid_part[:, RIM:]], 1)
            pg = jnp.concatenate([pg, pg_part[:, RIM:]], 1)
        else:
            hidden = jnp.concatenate([hid_part[:, : n - RIM], hidden], 1)
            pg = jnp.concatenate([pg_part[:, : n - RIM], pg], 1)
        pg_ref[...] = pg
        if even:
            kept_ref[...] = pg
            beside = (r_c[:, far_lanes], s_send[:, :RIM], s_send[:, RIM : 2 * RIM])
            for i, plane in enumerate(beside):
                block = slice(i * chans, (i + 1) * chans)
                two_ref[block, :] = two_part[block, :] + dot(far_hidden, plane, 1, 1)
            pack_two(send_ref, two_ref)
        else:
            kept_ref[...] = hidden
            beside = (s_send[:, n - 2 * RIM : n - RIM], s_send[:, n - RIM :], r_f[:, far_lanes])
            for i, plane in enumerate(beside):
                block = slice(i * chans, (i + 1) * chans)
                one_ref[:, block] = one_part[:, block] + dot(plane, far_pg, 1, 1)
            pack_one(send_ref, one_ref)
        near_plane, beyond = (n - RIM, 0) if even else (0, n + RIM)
        side_ref[:chans, :] = pre_ref[:, beyond : beyond + RIM]
        side_ref[chans:, :] = hg_ref[:, beyond : beyond + RIM]
        for i in range(RIM // (2 * chans)):
            lanes = slice(near_plane + 2 * i * chans, near_plane + 2 * (i + 1) * chans)
            send_ref[first + i * chans : first + (i + 1) * chans, :] = pg[:, lanes]

    @pl.when(odd_ref[0] % 2 == 0)
    def _():
        work(True, r_keep, r_send)

    @pl.when(odd_ref[0] % 2 != 0)
    def _():
        work(False, r_send, r_keep)


def far_plane(even, far_ref, side_ref, wf, wb, plane_ref, s_near, s_off):
    chans = plane_ref.shape[0]
    own, twice = slice(0, chans), slice(chans, 2 * chans)
    edge = slice(0, chans) if even else slice(2 * chans, 3 * chans)

    def terms(w, rows):
        write_shifts(s_near, far_ref[rows, :])
        write_shifts(s_off, far_ref[rows.start + 2 * chans : rows.stop + 2 * chans, :])
        return side_ref[rows, :] + dot(w[edge, :], s_off[...], 1, 0) + dot(w[twice, :], s_near[...], 1, 0)

    mask = far_ref[4 * chans : 4 * chans + 1, :].astype(F32)
    pre = terms(wf, own)
    _, plane_ref[...] = slope(terms(wb, twice), pre, mask)


def keep_kernel(odd_ref, s_keep, rims, kept_ref, far_ref, side_ref, wf, wb, keep_ref, plane_ref,
                one_ref, two_ref, s_near, s_off):
    @pl.when(odd_ref[0] % 2 == 0)
    def _():
        grad_one(keep_ref, s_keep, rims, kept_ref[...], one_ref)
        far_plane(True, far_ref, side_ref, wf, wb, plane_ref, s_near, s_off)

    @pl.when(odd_ref[0] % 2 != 0)
    def _():
        grad_two(keep_ref, s_keep, rims, kept_ref[...], two_ref)
        far_plane(False, far_ref, side_ref, wf, wb, plane_ref, s_near, s_off)


def pack_one(ref, one_ref):
    taps, chans = one_ref.shape[0], one_ref.shape[1] // 3
    fold = taps // 2
    ref[:taps, :] = one_ref[:, : 2 * chans].astype(ref.dtype)
    last = one_ref[:, 2 * chans :].astype(ref.dtype)
    ref[taps : taps + fold, :chans] = last[:fold]
    ref[taps : taps + fold, chans:] = last[fold:]


def pack_two(ref, two_ref):
    deep, chans = two_ref.shape[0], two_ref.shape[0] // 3
    fold = deep // 2
    for t in range(4):
        ref[t * deep : (t + 1) * deep, :] = two_ref[:, 2 * t * chans : 2 * (t + 1) * chans].astype(ref.dtype)
    last = two_ref[:, 8 * chans :].astype(ref.dtype)
    ref[4 * deep : 4 * deep + fold, :chans] = last[:fold]
    ref[4 * deep : 4 * deep + fold, chans:] = last[fold:]


def unpack_one(src, dst, dz):
    chans = dst.shape[1]
    taps = 9 * chans
    fold = taps // 2
    for j in range(9):
        first, k = j * chans, dz * 9 + j
        if dz < 2:
            dst[k] = src[first : first + chans, dz * chans : (dz + 1) * chans].astype(F32)
            continue
        for begin in range(first, first + chans, chans // 2):
            row, lane = taps + begin % fold, begin // fold * chans
            at = begin - first
            dst[k, at : at + chans // 2, :] = src[row : row + chans // 2, lane : lane + chans].astype(F32)


def unpack_two(src, dst, dz):
    chans = dst.shape[1]
    deep = 3 * chans
    fold = deep // 2
    first = (2 - dz) * chans
    for j in range(9):
        mirror, k = 8 - j, dz * 9 + j
        if mirror < 8:
            row, lane = mirror // 2 * deep + first, mirror % 2 * chans
            dst[k] = src[row : row + chans, lane : lane + chans].astype(F32)
            continue
        for begin in range(first, first + chans, chans // 2):
            row, lane = 4 * deep + begin % fold, begin // fold * chans
            at = begin - first
            dst[k, at : at + chans // 2, :] = src[row : row + chans // 2, lane : lane + chans].astype(F32)


def write_half(src, one_hbm, two_hbm, wide, sems, is_one):
    def write(unpack, out):
        copies = []
        for dz in range(3):
            unpack(src, wide, dz)
            third = pl.ds(dz * 9, 9)
            copies.append(pltpu.make_async_copy(wide.at[third], out.at[third], sems.at[dz]))
            copies[-1].start()
        for copy in copies:
            copy.wait()

    @pl.when(is_one)
    def _():
        write(unpack_one, one_hbm)

    @pl.when(jnp.logical_not(is_one))
    def _():
        write(unpack_two, two_hbm)


def join(joined, parts):
    first = 0
    for part in parts:
        joined[first : first + part.shape[0], :] = part[...]
        first += part.shape[0]


def mine_kernel(odd_ref, part, rest, one_hbm, two_hbm, joined, wide, sems):
    join(joined, (part, rest))
    write_half(joined, one_hbm, two_hbm, wide, sems, odd_ref[0] % 2 == 0)


def yours_kernel(odd_ref, part, rest, _one, _two, one_hbm, two_hbm, joined, wide, sems):
    join(joined, (part, rest))
    write_half(joined, one_hbm, two_hbm, wide, sems, odd_ref[0] % 2 != 0)


def last_kernel(odd_ref, near_ref, far_ref, m_ref, pg_ref, w1_hbm, _, out_ref, zero_ref, s_p, wb, w1, sems):
    chans, n = pg_ref.shape
    weights = pltpu.make_async_copy(w1_hbm, w1, sems.at[0])
    weights.start()
    zero_ref[...] = jnp.zeros_like(zero_ref)
    first = near_ref.shape[0] - RIM // 2
    near = jnp.concatenate(
        [near_ref[first + i * chans : first + (i + 1) * chans, :] for i in range(RIM // (2 * chans))], 1
    )
    left, right = sides(odd_ref, near, far_ref[...])
    write_shifts(s_p, jnp.concatenate([left, pg_ref[...], right], 1))
    weights.wait()
    backward_weights(w1, wb, chans)
    out = join_planes(dot(wb[...], s_p[...], 1, 0), chans) * m_ref[0:1, :].astype(F32)
    out_ref[...] = out.astype(BF)


def zeros_after(_, zero_ref):
    zero_ref[...] = jnp.zeros_like(zero_ref)


def whole(shape):
    return pl.BlockSpec(shape, lambda i: (0,) * len(shape))


HBM = pl.BlockSpec(memory_space=pltpu.HBM)
ANY = pl.BlockSpec(memory_space=pl.ANY)
SCALAR = pl.BlockSpec(memory_space=pltpu.SMEM)


def call(kernel, args, outs, scratch=(), specs=None, flops=0, out_specs=None, aliases=None):
    specs = specs or {}
    args = [
        pltpu.with_memory_space_constraint(x, pltpu.HBM) if specs.get(i) is HBM else x
        for i, x in enumerate(args)
    ]
    return pl.pallas_call(
        kernel,
        grid=(1,),
        in_specs=[specs.get(i, whole(x.shape)) for i, x in enumerate(args)],
        out_specs=out_specs or [whole(o.shape) for o in outs],
        input_output_aliases=aliases or {},
        out_shape=outs,
        scratch_shapes=list(scratch),
        compiler_params=pltpu.CompilerParams(vmem_limit_bytes=40 * 1024 * 1024),
        cost_estimate=pl.CostEstimate(flops=flops, bytes_accessed=0, transcendentals=0) if flops else None,
    )(*args)


def all_sum(keep, send, axis, beside):
    count = lax.axis_size(axis)
    bits = [1 << i for i in range(1, count.bit_length() - 1)]
    even_bits, odd_bits = bits, bits[-1:] + bits[:-1]

    def swap(x, step):
        bit = (even_bits[step], odd_bits[step])
        return lax.ppermute(x, axis, [(i, i ^ bit[i & 1]) for i in range(count)])

    def neighbour(x):
        return lax.ppermute(x, axis, [(i, i ^ 1) for i in range(count)])

    came = neighbour(send)
    rows = keep.shape[0]
    split = rows * 9 // 16 // 16 * 16
    whole_half = keep + came[:rows].astype(F32)
    parts = [whole_half[:split], whole_half[split:]]
    for step in range(len(bits)):
        for i, part in enumerate(parts):
            sent = part.astype(BF)
            other = swap(sent, step)
            if step == len(bits) - 1 and i == 0:
                zero = beside(came, sent)
            parts[i] = sent.astype(F32) + other.astype(F32)
    second = parts[1].astype(BF)
    near_second = neighbour(second)
    (later,) = call(zeros_after, (near_second,), [jax.ShapeDtypeStruct((8, keep.shape[1]), F32)], specs={0: ANY})
    first = (parts[0] + zero + later[:1]).astype(BF)
    return [first, second], [neighbour(first), near_second]


def far_partners(parts, count):
    pairs = []
    for part in range(parts):
        base = part * count
        for i in range(1, count - 1, 2):
            pairs += [(base + i, base + i + 1), (base + i + 1, base + i)]
        other = part ^ 1
        if other < parts:
            pairs += [(base, other * count), (base + count - 1, other * count + count - 1)]
    return pairs


def on_device(features, weight_one, weight_two, rules, cotangent):
    rows, chans = features.shape
    koff = rules.shape[1]
    ft, ct, rt = features.T, cotangent.T, rules.T
    count = lax.axis_size("slab")
    me = lax.axis_index("slab")
    inner = (me > 0) & (me < count - 1)
    odd = (me % 2 + 2 * inner.astype(me.dtype)).astype(jnp.int32).reshape(1)

    def array(*shape, kind=BF):
        return jax.ShapeDtypeStruct(shape, kind)

    def dma(n):
        return pltpu.SemaphoreType.DMA((n,))

    halo = (2 * chans, RIM)
    taps = 9 * chans
    weights = pltpu.VMEM(weight_one.shape, BF)
    near, far, f, c, m = call(
        prep_kernel,
        (odd, ft, ct, rt),
        [array(*halo), array(4 * chans + 16, RIM), array(chans, rows), array(chans, rows), array(16, rows)],
        [pltpu.VMEM((8, rows), jnp.int32), dma(3)],
        {0: SCALAR, 1: HBM, 2: HBM, 3: HBM},
    )
    far_pairs = far_partners(lax.axis_size("parts"), count)
    near_pairs = [(i, i ^ 1) for i in range(count)]
    near_in = lax.ppermute(near, "slab", near_pairs)
    far_in = lax.ppermute(far, ("parts", "slab"), far_pairs)
    s_keep, s_send, wf, wb, pre, hg = call(
        own_kernel,
        (odd, f, c, weight_one, weight_two),
        [array(taps, rows), array(taps, rows), array(3 * chans, taps), array(3 * chans, taps),
         array(chans, rows + 2 * RIM, kind=F32), array(chans, rows + 2 * RIM, kind=F32)],
        [weights, weights, pltpu.VMEM((taps, 3 * chans), BF), dma(2)],
        {0: SCALAR, 3: HBM, 4: HBM},
        flops=2 * 2 * rows * koff * chans * chans,
    )
    half = koff * chans // 2
    grad_scratch = [pltpu.VMEM((taps, 3 * chans), F32), pltpu.VMEM((3 * chans, taps), F32)]
    near_keep, near_send, hid, pg, one, two = call(
        near_kernel,
        (odd, near_in, m, wf, wb, pre, hg, s_send),
        [array(taps, RIM), array(taps, RIM), array(chans, rows), array(chans, rows),
         array(taps, 3 * chans, kind=F32), array(3 * chans, taps, kind=F32)],
        specs={0: SCALAR},
        flops=2 * RIM * koff * chans * chans,
    )
    send, side, pg, kept, rims = call(
        send_kernel,
        (odd, far_in, m, s_send, wf, wb, pre, hg, near_keep, near_send, hid, pg, one, two),
        [array(half + RIM // 2, 2 * chans), array(2 * chans, RIM, kind=F32), array(chans, rows), array(chans, rows),
         array(taps, 2 * RIM)],
        [pltpu.VMEM((taps, 2 * RIM), BF), *grad_scratch],
        {0: SCALAR},
        flops=2 * 2 * rows * koff * chans * chans,
    )
    keep, plane = call(
        keep_kernel,
        (odd, s_keep, rims, kept, far_in, side, wf, wb),
        [array(half, 2 * chans, kind=F32), array(chans, RIM)],
        [*grad_scratch, pltpu.VMEM((taps, RIM), BF), pltpu.VMEM((taps, RIM), BF)],
        {0: SCALAR},
        flops=2 * rows * koff * chans * chans,
    )
    done = []

    def beside(came, sent):
        fg, zero = call(
            last_kernel,
            (odd, came, plane, m, pg, weight_one, sent),
            [array(chans, rows), array(8, 2 * chans, kind=F32)],
            [pltpu.VMEM((taps, rows + 2 * RIM), BF), pltpu.VMEM((3 * chans, taps), BF), weights, dma(1)],
            {0: SCALAR, 5: HBM, 6: ANY},
            flops=2 * 2 * rows * koff * chans * chans,
        )
        done.append(fg)
        return zero[:1]

    mine, yours = all_sum(keep, send, "slab", beside)
    grads = [array(koff, chans, chans, kind=F32)] * 2
    scratch = [pltpu.VMEM((half, 2 * chans), BF), pltpu.VMEM((koff, chans, chans), F32), dma(3)]
    grads_out = call(
        mine_kernel, (odd, *mine), grads, scratch, {0: SCALAR}, flops=2 * rows * koff * chans * chans,
        out_specs=[ANY, ANY],
    )
    first_grad, second_grad = call(
        yours_kernel, (odd, *yours, *grads_out), grads, scratch, {0: SCALAR, 3: ANY, 4: ANY},
        out_specs=[ANY, ANY], aliases={3: 0, 4: 1},
    )
    return done[0].T, first_grad, second_grad


def solution(mesh):
    return jax.shard_map(
        on_device,
        mesh=mesh,
        in_specs=(
            P(("parts", "slab"), None),
            P(),
            P(),
            P(("parts", "slab"), None),
            P(("parts", "slab"), None),
        ),
        out_specs=(P(("parts", "slab"), None), P("parts", None, None), P("parts", None, None)),
        check_vma=False,
    )
```
